32 devices in a mesh: vertex: 16 (over z, y, x), view: 2 (over core).
Axes of the slice: x: 2, y: 2, z: 4, core: 2. Of those that a mesh axis runs over, the one named last changes fastest.
Arguments:
- coeffs: bfloat16 [512], P('view'), may hold values from -4 to 4
- shape_basis: bfloat16 [512, 3, 16384], P('view', None, 'vertex'), may hold values from -0.25 to 0.25
- rest_pose: float32 [3, 16384], P(None, 'vertex'), may hold values from -5 to 5
- triangles: int32 [3, 32768], P(None, 'vertex'), may hold values from 0 to 1023
- fetch_list: int32 [32, 16, 4], P(('vertex', 'view')), may hold values from -1 to 15, as said below
- tile_cover: int32 [1024, 8], P(('vertex', 'view')), may hold values from 0 to 63, as said below
- pix_slot: int32 [1024, 256], P(('vertex', 'view')), may hold values from 0 to 1023
- barycentric: float32 [1024, 3, 256], P(('vertex', 'view')), as said below
- camera: float32 [1024, 12], P(('vertex', 'view')), may hold values from -2 to 2
- target: float32 [1024, 3, 256], P(('vertex', 'view')), may hold values from -1 to 1
Outputs:
- photo_loss: float32 [], replicated
- vertex_grad: float32 [3, 16384], P(None, 'vertex')
- coeff_grad: float32 [512], P('view')
The draws below stay inside these ranges and needn't reach their ends.
Inputs may be any that keep to these rules, and one draw needn't show every extreme that they name: Triangle t lies in vertex shard t // 2048; its corners are the vertices triangles[c, t] + (t // 2048) * 1024 of that shard. Let u = o // 2 for owner o. Each row fetch_list[o, h] names distinct blocks of shard h, filled from the front and -1 after. A row is empty unless (h - u) mod 16 is one of j - 3 for j = 0 .. 8 - 2 (taken mod 16) or 8; other rows may be empty too, and every owner has some shard with all 4 entries filled. `tile_cover`: entry e of a tile names entry e % 4 of row e // 4 of the fetch list of the tile's owner (tile t belongs to owner t // 32); that entry is always filled. `pix_slot`: slot q names triangle q % 128 of the block given by the tile's coverage entry q // 128. `barycentric`: the three weights of a pixel are positive and sum to one.
All inputs are finite; a program needn't handle non-finite values.
Results may differ from the reference program's by a relative error of at most 0.0003.
Values sent between devices are 32-bit elements; how exact they have to be, the bound alone decides.
A program may use at most 64 MiB of HBM per device.

```python
import jax
import jax.numpy as jnp
from jax import lax

K = 512
V_DEV = 1024
BLOCK = 128
CAP = 4
WIN = 8
NB = 8
PIX = 256
TILE_DEV = 32
TB_DEV = 16
HOLDERS = 16
OWNERS = 32
VERTS = 16384
TRIS = 32768
TILES = 1024
PIXELS = 262144
N_VIEW = 2


def reach_table():
    window_ids = jnp.arange(WIN, dtype=jnp.int32)
    back = (WIN - 2) // 2
    return jnp.where(window_ids == WIN - 1, HOLDERS // 2, window_ids - back).astype(jnp.int32)


def request_counts(key):
    back = (WIN - 2) // 2
    window_counts = jax.random.randint(jax.random.fold_in(key, 101), (OWNERS, WIN), 0, CAP + 1)
    window_ids = jnp.arange(WIN, dtype=jnp.int32)[None, :]
    forced = (window_ids == WIN - 1) | (window_ids == back - 1)
    window_counts = jnp.where(forced, jnp.maximum(window_counts, 1), window_counts)
    full_at = jax.random.randint(jax.random.fold_in(key, 102), (OWNERS, 1), 0, WIN).astype(jnp.int32)
    window_counts = jnp.where(window_ids == full_at, CAP, window_counts).astype(jnp.int32)
    owner_vertex = (jnp.arange(OWNERS, dtype=jnp.int32) // (OWNERS // HOLDERS))[:, None]
    holder_ids = jnp.arange(HOLDERS, dtype=jnp.int32)[None, :]
    relative = (holder_ids - owner_vertex) % HOLDERS
    is_half = relative == HOLDERS // 2
    near_index = (relative + back) % HOLDERS
    window_index = jnp.where(is_half, WIN - 1, near_index)
    inside = is_half | (near_index < WIN - 1)
    picked = jnp.take_along_axis(window_counts, jnp.clip(window_index, 0, WIN - 1), axis=1)
    counts = jnp.where(inside, picked, 0).astype(jnp.int32)
    full_holder = ((owner_vertex + reach_table()[full_at]) % HOLDERS).astype(jnp.int32)
    return (counts, full_holder)


def draw_fetch_list(key, part):
    counts, full_holder = request_counts(key)
    scores = jax.random.randint(jax.random.fold_in(key, 103), (OWNERS, HOLDERS, TB_DEV), 0, 2 ** 16)
    scores = scores * TB_DEV + jnp.arange(TB_DEV, dtype=jnp.int32)
    ranked = jnp.argsort(scores, axis=-1)[:, :, :CAP].astype(jnp.int32)
    slot_ids = jnp.arange(CAP, dtype=jnp.int32)[None, None, :]
    return jnp.where(slot_ids < counts[:, :, None], ranked, -1).astype(jnp.int32)


def draw_tile_cover(key, part):
    back = (WIN - 2) // 2
    counts, full_holder = request_counts(key)
    tile_ids = jnp.arange(TILES, dtype=jnp.int32)
    owner_ids = tile_ids // TILE_DEV
    owner_vertex = owner_ids // (OWNERS // HOLDERS)
    pick_win = jax.random.randint(jax.random.fold_in(key, 104), (TILES, NB), 0, WIN).astype(jnp.int32)
    column_ids = jnp.arange(NB, dtype=jnp.int32)[None, :]
    first_tile = (tile_ids % TILE_DEV == 0)[:, None]
    pick_win = jnp.where(first_tile & (column_ids == 0), WIN - 1, pick_win)
    pick_win = jnp.where(first_tile & (column_ids == 1), back - 1, pick_win)
    pick_holder = (owner_vertex[:, None] + reach_table()[pick_win]) % HOLDERS
    available = counts[owner_ids[:, None], pick_holder]
    fallback = full_holder[owner_ids, 0][:, None]
    pick_holder = jnp.where(available > 0, pick_holder, fallback)
    available = jnp.where(available > 0, available, CAP)
    drawn = jax.random.randint(jax.random.fold_in(key, 105), (TILES, NB), 0, 2 ** 20)
    pick_slot = drawn % available
    return (pick_holder * CAP + pick_slot).astype(jnp.int32)


def draw_barycentric(key, part):
    uniform_raw = jax.random.uniform(key, (TILES, 3, PIX), jnp.float32, 0.05, 1.0)
    weights_raw = uniform_raw * uniform_raw + 0.02
    return weights_raw / jnp.sum(weights_raw, axis=1, keepdims=True)


def plant(array, own_key, smallest, high):
    index_at = [jax.random.randint(jax.random.fold_in(own_key, axis), (), 0, length) for axis, length in enumerate(array.shape)]
    widest = array.shape.index(max(array.shape))
    neighbour = index_at[:widest] + [(index_at[widest] + 1) % array.shape[widest]] + index_at[widest + 1:]
    return array.at[tuple(index_at)].set(smallest).at[tuple(neighbour)].set(high)


def block_scale(rng, dims, cuts, smallest, high):
    loudness = 1.0
    for dim, blocks in cuts:
        draws = jax.random.uniform(jax.random.fold_in(jax.random.fold_in(rng, 6), dim), (blocks,), jnp.float32, smallest / len(cuts), high / len(cuts))
        loudness = loudness * jnp.repeat(jnp.exp(draws), dims[dim] // blocks).reshape((-1,) + (1,) * (len(dims) - 1 - dim))
    return loudness


def centred(own_key, extent, scale, reach, cuts=(), kind=jnp.bfloat16):
    result = jax.random.normal(own_key, extent, jnp.float32) * scale
    if len(cuts) > 0:
        result = block_scale(own_key, extent, cuts, -0.22, 0.18) * result
    return jnp.clip(result, min=-reach, max=reach).astype(kind)


def setup_inputs(seed: int = 0) -> dict:
    splits = jax.random.split(jax.random.key(seed), 11)
    return {
        "coeffs": centred(splits[0], (K,), 1.0, 4.0, ((0, 2),)),
        "shape_basis": centred(splits[1], (K, 3, VERTS), K ** -0.5, 0.25, ((0, 2), (2, 16))),
        "rest_pose": centred(splits[2], (3, VERTS), 1.0, 5.0, ((1, 16),), jnp.float32),
        "triangles": plant(jax.random.randint(splits[3], (3, TRIS), 0, V_DEV), jax.random.fold_in(splits[3], 1), 0, V_DEV - 1).astype(jnp.int32),
        "fetch_list": draw_fetch_list(jax.random.fold_in(splits[10], 71), 0),
        "tile_cover": draw_tile_cover(jax.random.fold_in(splits[10], 71), 0),
        "pix_slot": plant(jax.random.randint(splits[6], (TILES, PIX), 0, NB * BLOCK), jax.random.fold_in(splits[6], 1), 0, (NB * BLOCK) - 1).astype(jnp.int32),
        "barycentric": draw_barycentric(jax.random.fold_in(splits[10], 71), 0),
        "camera": centred(splits[8], (TILES, 12), 0.4, 2.0, ((0, 32),), jnp.float32),
        "target": jnp.clip(jax.random.uniform(splits[9], (TILES, 3, PIX), jnp.float32, -1.0, 1.0) * block_scale(splits[9], (TILES, 3, PIX), ((0, 32),), -0.4, 0.0), -1.0, 1.0),
    }


SMOOTH = 0.1

def photometric(positions, triangles, fetch_list, tile_cover, pix_slot, barycentric, camera, target):
    tile_count = tile_cover.shape[0]
    owner_ids = (jnp.arange(tile_count, dtype=jnp.int32) // TILE_DEV)[:, None]
    entries = jnp.take_along_axis(tile_cover, pix_slot // BLOCK, axis=1)
    holder = entries // CAP
    local_block = fetch_list[owner_ids, holder, entries % CAP]
    triangle_ids = (holder * TB_DEV + local_block) * BLOCK + pix_slot % BLOCK
    surface = barycentric[None, :, 0, :] * positions[:, triangles[0, triangle_ids] + holder * V_DEV]
    surface = surface + barycentric[None, :, 1, :] * positions[:, triangles[1, triangle_ids] + holder * V_DEV]
    surface = surface + barycentric[None, :, 2, :] * positions[:, triangles[2, triangle_ids] + holder * V_DEV]
    matrix = camera[:, :9].reshape(tile_count, 3, 3)
    shifted = camera[:, 9:12]
    linear = matrix[:, :, 0, None] * surface[0][:, None, :]
    linear = linear + matrix[:, :, 1, None] * surface[1][:, None, :]
    linear = linear + matrix[:, :, 2, None] * surface[2][:, None, :]
    linear = linear + shifted[:, :, None]
    shaded = jnp.tanh(linear)
    differ = shaded - target
    return jnp.sum(jnp.sqrt(differ * differ + SMOOTH * SMOOTH))

def reference(coeffs, shape_basis, rest_pose, triangles, fetch_list, tile_cover, pix_slot, barycentric, camera, target):
    flat_basis = shape_basis.reshape(K, 3 * VERTS)
    offset = jnp.dot(coeffs[None, :], flat_basis, preferred_element_type=jnp.float32).reshape(3, VERTS)
    positions = rest_pose + offset
    energy, vertex_grad = jax.value_and_grad(photometric)(positions, triangles, fetch_list, tile_cover, pix_slot, barycentric, camera, target)
    groups = flat_basis.reshape(N_VIEW, K // N_VIEW, 3 * VERTS)
    flat_grad = vertex_grad.reshape(3 * VERTS)

    def project(basis_rows):
        return jnp.dot(basis_rows.astype(jnp.float32), flat_grad, precision=lax.Precision.HIGHEST)
    coeff_grad = lax.map(project, groups).reshape(K)
    return (energy / PIXELS, vertex_grad, coeff_grad)
```

```python
import functools

import jax
import jax.numpy as jnp
from jax import lax
from jax.experimental import pallas as pl
from jax.experimental.pallas import tpu as pltpu
from jax.sharding import PartitionSpec as P

MESH = pl.DeviceIdType.MESH
BLOCK = 128
LANES = 128
WIN = 8
BACK = 3
SMOOTH = 0.1
F32 = jnp.float32
BF16 = jnp.bfloat16
NT = (((1,), (1,)), ((), ()))
TN = (((0,), (0,)), ((), ()))


def reach(j, holders):
    return holders // 2 if j == WIN - 1 else j - BACK


def pick_lanes(table, lanes):
    return jnp.take_along_axis(table, lanes, axis=1, mode="promise_in_bounds")


def two_parts(values):
    high = values.astype(BF16)
    low = (values - high.astype(F32)).astype(BF16)
    return high, low


def three_parts(values):
    high = values.astype(BF16)
    rest = values - high.astype(F32)
    middle = rest.astype(BF16)
    low = (rest - middle.astype(F32)).astype(BF16)
    return high, middle, low


def kernel(
    nh, nv, pixel_total,
    coeffs_ref, basis_ref, rest_ref, tri_ref, fetch_ref, cover_ref, slot_ref, bary_ref, cam_ref,
    target_ref,
    loss_ref, vgrad_ref, coeff_ref,
    basis_v, part, rest_rows, pos_all, tri_all, ids_ref, table, cover_row, rows_ref, cam_t,
    corner_grad, rows_grad, energy_ref, grad_table, grad_out, grad_in, view_in, coeff_in,
    basis_sem, tri_send, tri_recv, part_send, part_recv, pos_send, pos_recv, grad_send, grad_recv,
    view_send, view_recv, coeff_send, coeff_recv,
):
    u = lax.axis_index("vertex")
    v = lax.axis_index("view")
    nk = basis_v.shape[1]
    his = rest_ref.shape[1] // LANES
    comps = 3 * his
    tiles = slot_ref.shape[0]
    pix = slot_ref.shape[1]
    covers = cover_ref.shape[0]
    caps = fetch_ref.shape[0]
    live = WIN * caps
    window = [j for j in range(WIN) if j != BACK]

    def at_vertex(step):
        return lax.rem(u + step + nh, nh)

    def at_view(step):
        return lax.rem(v + step, nv)

    barrier = pltpu.get_barrier_semaphore()
    for r in range(1, nh):
        pl.semaphore_signal(barrier, inc=1, device_id=(at_vertex(r), v), device_id_type=MESH)
    for r in range(1, nv):
        pl.semaphore_signal(barrier, inc=1, device_id=(u, at_view(r)), device_id_type=MESH)

    loads = [
        pltpu.make_async_copy(basis_ref.at[d], basis_v.at[d], basis_sem.at[d]) for d in range(3)
    ]
    for load in loads:
        load.start()
    tri_all[BACK] = tri_ref[...]

    pl.semaphore_wait(barrier, nh + nv - 2)

    tri_copies = {}
    for j in window:
        tri_copies[j] = pltpu.make_async_remote_copy(
            src_ref=tri_ref, dst_ref=tri_all.at[j], send_sem=tri_send.at[j],
            recv_sem=tri_recv.at[j], device_id=(at_vertex(-reach(j, nh)), v), device_id_type=MESH,
        )
        tri_copies[j].start()

    for d in range(3):
        loads[d].wait()
        share = jnp.dot(coeffs_ref[...], basis_v[d], preferred_element_type=F32)
        for i in range(his):
            part[v, pl.ds(d * his + i, 1), :] = share[:, i * LANES : (i + 1) * LANES]
            rest_rows[d * his + i : d * his + i + 1, :] = rest_ref[
                d : d + 1, i * LANES : (i + 1) * LANES
            ]

    def view_copies(buffer, send, recv):
        out = []
        for r in range(1, nv):
            out.append(
                pltpu.make_async_remote_copy(
                    src_ref=buffer.at[v], dst_ref=buffer.at[v], send_sem=send.at[r],
                    recv_sem=recv.at[v], device_id=(u, at_view(r)), device_id_type=MESH,
                )
            )
        return out

    def wait_views(buffer, recv):
        for r in range(1, nv):
            other = at_view(r)
            pltpu.make_async_remote_copy(
                src_ref=buffer.at[other], dst_ref=buffer.at[other], send_sem=recv.at[other],
                recv_sem=recv.at[other], device_id=(u, other), device_id_type=MESH,
            ).wait_recv()

    part_copies = view_copies(part, part_send, part_recv)
    for copy in part_copies:
        copy.start()

    entry = cover_ref[...]
    holder = entry // caps
    away = holder - u
    away = jnp.where(away < 0, away + nh, away)
    near = jnp.where(away <= BACK, away + BACK, away + BACK - nh)
    compact = jnp.where(away == nh // 2, WIN - 1, near) * caps + entry % caps
    for n in range(covers):
        cover_row[0:1, n * tiles : (n + 1) * tiles] = compact[n : n + 1, :]
    entry_ids = lax.broadcasted_iota(jnp.int32, (live, covers * tiles), 0)
    pick = (entry_ids == cover_row[...]).astype(F32).astype(BF16)
    cam_t[...] = jnp.transpose(cam_ref[...])

    wait_views(part, part_recv)
    total = part[0]
    for other in range(1, nv):
        total = total + part[other]
    pos_all[BACK] = rest_rows[...] + total
    pos_copies = {}
    for j in window:
        pos_copies[j] = pltpu.make_async_remote_copy(
            src_ref=pos_all.at[BACK], dst_ref=pos_all.at[j], send_sem=pos_send.at[j],
            recv_sem=pos_recv.at[j], device_id=(at_vertex(-reach(j, nh)), v), device_id_type=MESH,
        )
        pos_copies[j].start()

    for j in window:
        tri_copies[j].wait_recv()
    blocks = tri_ref.shape[1] // BLOCK
    for j in range(WIN):
        wanted = [
            jnp.full((3, BLOCK), fetch_ref[s, at_vertex(reach(j, nh))], jnp.int32)
            for s in range(caps)
        ]
        found = [jnp.zeros((3, BLOCK), jnp.int32)] * caps
        for b in range(blocks):
            corners = tri_all[j, :, b * BLOCK : (b + 1) * BLOCK]
            for s in range(caps):
                found[s] = jnp.where(wanted[s] == b, corners, found[s])
        for s in range(caps):
            for c in range(3):
                ids_ref[c, j * caps + s : j * caps + s + 1, :] = found[s][c : c + 1, :]

    for j in window:
        pos_copies[j].wait_recv()

    sub8 = lax.broadcasted_iota(jnp.int32, (8, LANES), 0)
    shards = 8 // caps
    for q in range(live // 8):
        ids = [ids_ref[c, 8 * q : 8 * q + 8, :] for c in range(3)]
        lows = [x % LANES for x in ids]
        highs = [x // LANES for x in ids]
        for d in range(3):
            picked = [jnp.zeros((8, LANES), F32)] * 3
            for i in range(his):
                source = None
                for w in range(shards):
                    row = jnp.broadcast_to(
                        pos_all[q * shards + w, d * his + i : d * his + i + 1, :], (8, LANES)
                    )
                    source = row if source is None else jnp.where(sub8 >= w * caps, row, source)
                for c in range(3):
                    picked[c] = jnp.where(highs[c] == i, pick_lanes(source, lows[c]), picked[c])
            for c in range(3):
                k = c * 3 + d
                table[8 * q : 8 * q + 8, k * LANES : (k + 1) * LANES] = picked[c]

    pick3 = jnp.concatenate([pick, pick, pick], axis=0)
    parts = jnp.concatenate(three_parts(table[...]), axis=0)
    rows_ref[...] = lax.dot_general(pick3, parts, TN, preferred_element_type=F32)

    energy_ref[...] = jnp.zeros((8, LANES), F32)

    def shade(g, carry):
        base = pl.multiple_of(g * 8, 8)
        lens = [cam_t[pl.ds(base, 8), i : i + 1] for i in range(12)]
        for half in range(pix // LANES):
            span = slice(half * LANES, (half + 1) * LANES)
            slots = slot_ref[pl.ds(base, 8), span]
            lanes = slots % BLOCK
            where_n = slots // BLOCK
            masks = [where_n == n for n in range(covers)]
            corners = []
            for k in range(9):
                picked = jnp.zeros((8, LANES), F32)
                for n in range(covers):
                    source = rows_ref[
                        pl.ds(pl.multiple_of(n * tiles + base, 8), 8), k * LANES : (k + 1) * LANES
                    ]
                    picked = jnp.where(masks[n], pick_lanes(source, lanes), picked)
                corners.append(picked)
            weights = [bary_ref[c, pl.ds(base, 8), span] for c in range(3)]
            surface = []
            for d in range(3):
                point = weights[0] * corners[d]
                point = point + weights[1] * corners[3 + d]
                surface.append(point + weights[2] * corners[6 + d])
            energy = energy_ref[...]
            grads = []
            for r in range(3):
                linear = lens[3 * r] * surface[0]
                linear = linear + lens[3 * r + 1] * surface[1]
                linear = linear + lens[3 * r + 2] * surface[2]
                shaded = jnp.tanh(linear + lens[9 + r])
                differ = shaded - target_ref[r, pl.ds(base, 8), span]
                spread = jnp.sqrt(differ * differ + SMOOTH * SMOOTH)
                energy = energy + spread
                grads.append(differ / spread * (1.0 - shaded * shaded))
            energy_ref[...] = energy
            for d in range(3):
                pull = lens[d] * grads[0] + lens[3 + d] * grads[1] + lens[6 + d] * grads[2]
                for c in range(3):
                    corner_grad[c * 3 + d, pl.ds(base, 8), span] = weights[c] * pull
        return carry

    lax.fori_loop(0, tiles // 8, shade, 0)

    lane_ids = lax.broadcasted_iota(jnp.int32, (BLOCK, pix), 0)
    cover_ids = lax.broadcasted_iota(jnp.int32, (covers, pix), 0)

    def spread_tile(t, carry):
        slots = slot_ref[pl.ds(t, 1), :]
        onehot = (lane_ids == slots % BLOCK).astype(F32).astype(BF16)
        mine = cover_ids == slots // BLOCK
        wide = jnp.concatenate(
            [jnp.where(mine, corner_grad[k, pl.ds(t, 1), :], 0.0) for k in range(9)], axis=0
        )
        both = jnp.concatenate(two_parts(wide), axis=0)
        summed = lax.dot_general(both, onehot, NT, preferred_element_type=F32)
        summed = summed[0 : 9 * covers] + summed[9 * covers :]
        for k in range(9):
            rows_grad[k, pl.ds(t, covers, stride=tiles), :] = summed[k * covers : (k + 1) * covers]
        return carry

    lax.fori_loop(0, tiles, spread_tile, 0, unroll=4)

    pick2 = jnp.concatenate([pick, pick], axis=1)
    for k in range(9):
        both = jnp.concatenate(two_parts(rows_grad[k]), axis=0)
        grad_table[k] = jnp.dot(pick2, both, preferred_element_type=F32)

    low_ids = lax.broadcasted_iota(jnp.int32, (LANES, LANES), 0)
    high_ids = lax.broadcasted_iota(jnp.int32, (his, LANES), 0)

    def spread_shard(j, carry):
        summed = jnp.zeros((2 * comps, LANES), F32)
        for s in range(caps):
            e = j * caps + s
            wide = []
            onehot = []
            for c in range(3):
                ids = ids_ref[c, pl.ds(e, 1), :]
                onehot.append((low_ids == ids % LANES).astype(F32).astype(BF16))
                mine = high_ids == ids // LANES
                wide.append(
                    jnp.concatenate(
                        [
                            jnp.where(
                                mine,
                                grad_table[c * 3 + d, pl.ds(e, 1), :],
                                0.0,
                            )
                            for d in range(3)
                        ],
                        axis=0,
                    )
                )
            high, low = two_parts(jnp.concatenate(wide, axis=1))
            summed = summed + lax.dot_general(
                jnp.concatenate([high, low], axis=0), jnp.concatenate(onehot, axis=1), NT,
                preferred_element_type=F32,
            )
        grad_out[j] = summed[0:comps] + summed[comps:]
        return carry

    lax.fori_loop(0, WIN, spread_shard, 0, unroll=2)

    grad_copies = {}
    for j in window:
        grad_copies[j] = pltpu.make_async_remote_copy(
            src_ref=grad_out.at[j], dst_ref=grad_in.at[j], send_sem=grad_send.at[j],
            recv_sem=grad_recv.at[j], device_id=(at_vertex(reach(j, nh)), v), device_id_type=MESH,
        )
        grad_copies[j].start()
    gathered = grad_out[BACK]
    for j in window:
        grad_copies[j].wait_recv()
        gathered = gathered + grad_in[j]
    view_in[v, 0:comps, :] = gathered
    view_in[v, comps : comps + 8, :] = energy_ref[...]
    out_copies = view_copies(view_in, view_send, view_recv)
    for copy in out_copies:
        copy.start()
    wait_views(view_in, view_recv)
    total = view_in[0]
    for other in range(1, nv):
        total = total + view_in[other]
    for d in range(3):
        for i in range(his):
            vgrad_ref[d : d + 1, i * LANES : (i + 1) * LANES] = total[
                d * his + i : d * his + i + 1, :
            ]

    share = jnp.zeros((2, nk), F32)
    for d in range(3):
        whole = vgrad_ref[d : d + 1, :]
        high = whole.astype(BF16).astype(F32)
        both = jnp.concatenate([high, whole - high], axis=0).astype(BF16)
        share = share + lax.dot_general(both, basis_v[d], NT, preferred_element_type=F32)
    share = share[0:1] + share[1:2]
    wide = min(nk, LANES)
    rows = nk // wide
    coeff_in[u] = jnp.zeros((8, LANES), F32)
    for i in range(rows):
        coeff_in[u, i : i + 1, 0:wide] = share[:, i * wide : (i + 1) * wide]
    coeff_in[u, rows : rows + 1, :] = jnp.sum(total[comps : comps + 8], axis=0, keepdims=True)
    coeff_copies = []
    for r in range(1, nh):
        coeff_copies.append(
            pltpu.make_async_remote_copy(
                src_ref=coeff_in.at[u], dst_ref=coeff_in.at[u], send_sem=coeff_send.at[r],
                recv_sem=coeff_recv.at[u], device_id=(at_vertex(r), v), device_id_type=MESH,
            )
        )
        coeff_copies[-1].start()

    for copies in (tri_copies, pos_copies, grad_copies):
        for j in window:
            copies[j].wait_send()
    for copy in part_copies + out_copies:
        copy.wait_send()
    for r in range(1, nh):
        other = at_vertex(r)
        pltpu.make_async_remote_copy(
            src_ref=coeff_in.at[other], dst_ref=coeff_in.at[other], send_sem=coeff_recv.at[other],
            recv_sem=coeff_recv.at[other], device_id=(other, v), device_id_type=MESH,
        ).wait_recv()
    total = coeff_in[0]
    for other in range(1, nh):
        total = total + coeff_in[other]
    for i in range(rows):
        coeff_ref[:, i * wide : (i + 1) * wide] = total[i : i + 1, 0:wide]
    loss_ref[...] = jnp.sum(total[rows : rows + 1, :], axis=1, keepdims=True) / pixel_total
    for copy in coeff_copies:
        copy.wait_send()


def per_device(
    nh, nv, coeffs, shape_basis, rest_pose, triangles, fetch_list, tile_cover, pix_slot,
    barycentric, camera, target,
):
    nk, _, verts = shape_basis.shape
    tiles, pix = pix_slot.shape
    covers = tile_cover.shape[1]
    caps = fetch_list.shape[2]
    live = WIN * caps
    comps = 3 * verts // LANES
    vmem = pl.BlockSpec(memory_space=pltpu.VMEM)
    smem = pl.BlockSpec(memory_space=pltpu.SMEM)
    hbm = pl.BlockSpec(memory_space=pl.ANY)
    dma = pltpu.SemaphoreType.DMA
    loss, vertex_grad, coeff_grad = pl.pallas_call(
        functools.partial(kernel, nh, nv, float(tiles * pix * nh * nv)),
        out_shape=(
            jax.ShapeDtypeStruct((1, 1), F32),
            jax.ShapeDtypeStruct((3, verts), F32),
            jax.ShapeDtypeStruct((1, nk), F32),
        ),
        in_specs=[vmem, hbm, vmem, vmem, smem, vmem, vmem, vmem, vmem, vmem],
        out_specs=(vmem, vmem, vmem),
        scratch_shapes=[
            pltpu.VMEM((3, nk, verts), BF16),
            pltpu.VMEM((nv, comps, LANES), F32),
            pltpu.VMEM((comps, LANES), F32),
            pltpu.VMEM((WIN, comps, LANES), F32),
            pltpu.VMEM((WIN,) + triangles.shape, jnp.int32),
            pltpu.VMEM((3, live, LANES), jnp.int32),
            pltpu.VMEM((live, 9 * LANES), F32),
            pltpu.VMEM((1, covers * tiles), jnp.int32),
            pltpu.VMEM((covers * tiles, 9 * LANES), F32),
            pltpu.VMEM((tiles, 12), F32),
            pltpu.VMEM((9, tiles, pix), F32),
            pltpu.VMEM((9, covers * tiles, LANES), F32),
            pltpu.VMEM((8, LANES), F32),
            pltpu.VMEM((9, live, LANES), F32),
            pltpu.VMEM((WIN, comps, LANES), F32),
            pltpu.VMEM((WIN, comps, LANES), F32),
            pltpu.VMEM((nv, comps + 8, LANES), F32),
            pltpu.VMEM((nh, 8, LANES), F32),
            dma((3,)),
            dma((WIN,)), dma((WIN,)),
            dma((nv,)), dma((nv,)),
            dma((WIN,)), dma((WIN,)),
            dma((WIN,)), dma((WIN,)),
            dma((nv,)), dma((nv,)),
            dma((nh,)), dma((nh,)),
        ],
        compiler_params=pltpu.CompilerParams(
            collective_id=0, has_side_effects=True, vmem_limit_bytes=40 * 1024 * 1024
        ),
    )(
        coeffs.reshape(1, nk),
        jnp.transpose(shape_basis, (1, 0, 2)),
        rest_pose,
        triangles,
        jnp.transpose(fetch_list[0], (1, 0)),
        jnp.transpose(tile_cover, (1, 0)),
        pix_slot,
        jnp.transpose(barycentric, (1, 0, 2)),
        jnp.transpose(camera, (1, 0)),
        jnp.transpose(target, (1, 0, 2)),
    )
    return loss.reshape(()), vertex_grad, coeff_grad.reshape(nk)


def solution(mesh):
    placed = (
        P("view"),
        P("view", None, "vertex"),
        P(None, "vertex"),
        P(None, "vertex"),
        P(("vertex", "view"), None, None),
        P(("vertex", "view"), None),
        P(("vertex", "view"), None),
        P(("vertex", "view"), None, None),
        P(("vertex", "view"), None),
        P(("vertex", "view"), None, None),
    )
    return jax.shard_map(
        functools.partial(per_device, mesh.shape["vertex"], mesh.shape["view"]),
        mesh=mesh,
        in_specs=placed,
        out_specs=(P(), P(None, "vertex"), P("view")),
        check_vma=False,
    )
```

```python
import functools

import jax
import jax.numpy as jnp
from jax import lax
from jax.experimental import pallas as pl
from jax.experimental.pallas import tpu as pltpu
from jax.sharding import PartitionSpec as P

MESH = pl.DeviceIdType.MESH
BLOCK = 128
LANES = 128
WIN = 8
BACK = 3
SMOOTH = 0.1
F32 = jnp.float32
BF16 = jnp.bfloat16
NT = (((1,), (1,)), ((), ()))
TN = (((0,), (0,)), ((), ()))


def reach(j, holders):
    return holders // 2 if j == WIN - 1 else j - BACK


def pick_lanes(table, lanes):
    return jnp.take_along_axis(table, lanes, axis=1, mode="promise_in_bounds")


def two_parts(values):
    high = values.astype(BF16)
    low = (values - high.astype(F32)).astype(BF16)
    return high, low


def three_parts(values):
    high = values.astype(BF16)
    rest = values - high.astype(F32)
    middle = rest.astype(BF16)
    low = (rest - middle.astype(F32)).astype(BF16)
    return high, middle, low


def kernel(
    nh, nv, pixel_total,
    coeffs_in, basis_in, rest_in, tri_ref, fetch_in, cover_in, slot_in, bary_in, cam_in, target_in,
    loss_ref, vgrad_ref, coeff_ref,
    coeffs_ref, basis_v, rest_ref, fetch_ref, cover_ref, slot_ref, bary_ref, cam_ref, target_ref,
    tile_hot, vert_hot, part, rest_rows, pos_all, tri_all, ids_ref, table, cover_row, rows_ref, cam_t,
    corner_grad, rows_grad, energy_ref, grad_table, grad_out, grad_in, view_in, coeff_in,
    load_sem, tri_send, tri_recv, part_send, part_recv, pos_send, pos_recv, grad_send, grad_recv,
    view_send, view_recv, coeff_send, coeff_recv,
):
    u = lax.axis_index("vertex")
    v = lax.axis_index("view")
    nk = basis_v.shape[1]
    his = rest_ref.shape[1] // LANES
    comps = 3 * his
    tiles = slot_ref.shape[0]
    pix = slot_ref.shape[1]
    covers = cover_ref.shape[0]
    caps = fetch_ref.shape[0]
    cap_bits = caps.bit_length() - 1
    live = WIN * caps
    window = [j for j in range(WIN) if j != BACK]

    def at_vertex(step):
        return lax.rem(u + step + nh, nh)

    def at_view(step):
        return lax.rem(v + step, nv)

    pairs = [
        (coeffs_in, coeffs_ref), (basis_in.at[0], basis_v.at[0]), (basis_in.at[1], basis_v.at[1]),
        (basis_in.at[2], basis_v.at[2]), (rest_in, rest_ref), (cover_in, cover_ref),
        (cam_in, cam_ref), (slot_in, slot_ref), (fetch_in, fetch_ref), (tri_ref, tri_all.at[BACK]),
        (bary_in, bary_ref), (target_in, target_ref),
    ]
    loads = [
        pltpu.make_async_copy(src, dst, load_sem.at[i]) for i, (src, dst) in enumerate(pairs)
    ]
    for load in loads[:4]:
        load.start()

    barrier = pltpu.get_barrier_semaphore()
    for r in range(1, nv):
        pl.semaphore_signal(barrier, inc=1, device_id=(u, at_view(r)), device_id_type=MESH)
    for r in range(1, nh):
        pl.semaphore_signal(barrier, inc=1, device_id=(at_vertex(r), v), device_id_type=MESH)
    for load in loads[4:]:
        load.start()

    loads[0].wait()
    for d in range(3):
        loads[1 + d].wait()
        share = jnp.dot(coeffs_ref[...].reshape(1, nk), basis_v[d], preferred_element_type=F32)
        for i in range(his):
            part[v, pl.ds(d * his + i, 1), :] = share[:, i * LANES : (i + 1) * LANES]

    pl.semaphore_wait(barrier, nh + nv - 2)

    def view_copies(buffer, send, recv):
        out = []
        for r in range(1, nv):
            out.append(
                pltpu.make_async_remote_copy(
                    src_ref=buffer.at[v], dst_ref=buffer.at[v], send_sem=send.at[r],
                    recv_sem=recv.at[v], device_id=(u, at_view(r)), device_id_type=MESH,
                )
            )
        return out

    def wait_views(buffer, recv):
        for r in range(1, nv):
            other = at_view(r)
            pltpu.make_async_remote_copy(
                src_ref=buffer.at[other], dst_ref=buffer.at[other], send_sem=recv.at[other],
                recv_sem=recv.at[other], device_id=(u, other), device_id_type=MESH,
            ).wait_recv()

    part_copies = view_copies(part, part_send, part_recv)
    for copy in part_copies:
        copy.start()
    tri_copies = {}
    for j in window:
        tri_copies[j] = pltpu.make_async_remote_copy(
            src_ref=tri_ref, dst_ref=tri_all.at[j], send_sem=tri_send.at[j],
            recv_sem=tri_recv.at[j], device_id=(at_vertex(-reach(j, nh)), v), device_id_type=MESH,
        )
        tri_copies[j].start()

    for load in loads[4:8]:
        load.wait()
    for d in range(3):
        for i in range(his):
            rest_rows[d * his + i : d * his + i + 1, :] = rest_ref[
                d : d + 1, i * LANES : (i + 1) * LANES
            ]
    entry = cover_ref[...]
    holder = entry >> cap_bits
    away = holder - u
    away = jnp.where(away < 0, away + nh, away)
    near = jnp.where(away <= BACK, away + BACK, away + BACK - nh)
    compact = jnp.where(away == nh // 2, WIN - 1, near) * caps + (entry & (caps - 1))
    for n in range(covers):
        cover_row[0:1, n * tiles : (n + 1) * tiles] = compact[n : n + 1, :]
    entry_ids = lax.broadcasted_iota(jnp.int32, (live, covers * tiles), 0)
    pick = (entry_ids == cover_row[...]).astype(F32).astype(BF16)
    cam_t[...] = jnp.transpose(cam_ref[...])

    lane_ids = lax.broadcasted_iota(jnp.int32, (BLOCK, pix), 0)

    def tile_lanes(t, carry):
        lanes = slot_ref[pl.ds(t, 1), :] & (BLOCK - 1)
        tile_hot[t] = (lane_ids == lanes).astype(F32).astype(BF16)
        return carry

    wait_views(part, part_recv)
    total = part[0]
    for other in range(1, nv):
        total = total + part[other]
    pos_all[BACK] = rest_rows[...] + total
    pos_copies = {}
    for j in window:
        pos_copies[j] = pltpu.make_async_remote_copy(
            src_ref=pos_all.at[BACK], dst_ref=pos_all.at[j], send_sem=pos_send.at[j],
            recv_sem=pos_recv.at[j], device_id=(at_vertex(-reach(j, nh)), v), device_id_type=MESH,
        )
        pos_copies[j].start()

    lax.fori_loop(0, tiles, tile_lanes, 0, unroll=4)
    loads[8].wait()
    loads[9].wait()
    for j in window:
        tri_copies[j].wait_recv()
    blocks = tri_ref.shape[1] // BLOCK
    for j in range(WIN):
        wanted = [
            jnp.full((3, BLOCK), fetch_ref[s, at_vertex(reach(j, nh))], jnp.int32)
            for s in range(caps)
        ]
        found = [jnp.zeros((3, BLOCK), jnp.int32)] * caps
        for b in range(blocks):
            corners = tri_all[j, :, b * BLOCK : (b + 1) * BLOCK]
            for s in range(caps):
                found[s] = jnp.where(wanted[s] == b, corners, found[s])
        for s in range(caps):
            for c in range(3):
                ids_ref[c, j * caps + s : j * caps + s + 1, :] = found[s][c : c + 1, :]

    low_ids = lax.broadcasted_iota(jnp.int32, (LANES, LANES), 0)

    def vertex_lanes(e, carry):
        for c in range(3):
            lows = ids_ref[c, pl.ds(e, 1), :] & (LANES - 1)
            vert_hot[e, :, c * LANES : (c + 1) * LANES] = (
                (low_ids == lows).astype(F32).astype(BF16)
            )
        return carry

    lax.fori_loop(0, live, vertex_lanes, 0, unroll=2)

    for j in window:
        pos_copies[j].wait_recv()

    sub8 = lax.broadcasted_iota(jnp.int32, (8, LANES), 0)
    shards = 8 // caps
    for q in range(live // 8):
        ids = [ids_ref[c, 8 * q : 8 * q + 8, :] for c in range(3)]
        lows = [x & (LANES - 1) for x in ids]
        highs = [x >> 7 for x in ids]
        sources = []
        for row in range(comps):
            source = None
            for w in range(shards):
                wide = jnp.broadcast_to(pos_all[q * shards + w, row : row + 1, :], (8, LANES))
                source = wide if source is None else jnp.where(sub8 >= w * caps, wide, source)
            sources.append(source)
        for c in range(3):
            masks = [highs[c] == i for i in range(his)]
            for d in range(3):
                picked = jnp.zeros((8, LANES), F32)
                for i in range(his):
                    picked = jnp.where(masks[i], pick_lanes(sources[d * his + i], lows[c]), picked)
                k = c * 3 + d
                table[8 * q : 8 * q + 8, k * LANES : (k + 1) * LANES] = picked

    pick3 = jnp.concatenate([pick, pick, pick], axis=0)
    parts = jnp.concatenate(three_parts(table[...]), axis=0)
    rows_ref[...] = lax.dot_general(pick3, parts, TN, preferred_element_type=F32)

    energy_ref[...] = jnp.zeros((8, LANES), F32)
    loads[10].wait()
    loads[11].wait()

    def shade(g, carry):
        base = pl.multiple_of(g * 8, 8)
        lens = [cam_t[pl.ds(base, 8), i : i + 1] for i in range(12)]
        for half in range(pix // LANES):
            span = slice(half * LANES, (half + 1) * LANES)
            slots = slot_ref[pl.ds(base, 8), span]
            lanes = slots & (BLOCK - 1)
            where_n = slots >> 7
            masks = [where_n == n for n in range(covers)]
            corners = []
            for k in range(9):
                picked = jnp.zeros((8, LANES), F32)
                for n in range(covers):
                    source = rows_ref[
                        pl.ds(pl.multiple_of(n * tiles + base, 8), 8), k * LANES : (k + 1) * LANES
                    ]
                    picked = jnp.where(masks[n], pick_lanes(source, lanes), picked)
                corners.append(picked)
            weights = [bary_ref[c, pl.ds(base, 8), span] for c in range(3)]
            surface = []
            for d in range(3):
                point = weights[0] * corners[d]
                point = point + weights[1] * corners[3 + d]
                surface.append(point + weights[2] * corners[6 + d])
            energy = energy_ref[...]
            grads = []
            for r in range(3):
                linear = lens[3 * r] * surface[0]
                linear = linear + lens[3 * r + 1] * surface[1]
                linear = linear + lens[3 * r + 2] * surface[2]
                shaded = jnp.tanh(linear + lens[9 + r])
                differ = shaded - target_ref[r, pl.ds(base, 8), span]
                square = differ * differ + SMOOTH * SMOOTH
                inverse = lax.rsqrt(square)
                energy = energy + square * inverse
                grads.append(differ * inverse * (1.0 - shaded * shaded))
            energy_ref[...] = energy
            for d in range(3):
                pull = lens[d] * grads[0] + lens[3 + d] * grads[1] + lens[6 + d] * grads[2]
                for c in range(3):
                    value = weights[c] * pull
                    high = value.astype(BF16).astype(F32)
                    corner_grad[c * 3 + d, pl.ds(base, 8), span] = high
                    corner_grad[9 + c * 3 + d, pl.ds(base, 8), span] = value - high
        return carry

    lax.fori_loop(0, tiles // 8, shade, 0)

    cover_ids = lax.broadcasted_iota(jnp.int32, (covers, pix), 0)

    def spread_tile(t, carry):
        mine = cover_ids == (slot_ref[pl.ds(t, 1), :] >> 7)
        both = jnp.concatenate(
            [jnp.where(mine, corner_grad[k, pl.ds(t, 1), :], 0.0) for k in range(18)], axis=0
        ).astype(BF16)
        summed = lax.dot_general(both, tile_hot[t], NT, preferred_element_type=F32)
        summed = summed[0 : 9 * covers] + summed[9 * covers :]
        for k in range(9):
            rows_grad[k, pl.ds(t, covers, stride=tiles), :] = summed[k * covers : (k + 1) * covers]
        return carry

    lax.fori_loop(0, tiles, spread_tile, 0, unroll=4)

    pick2 = jnp.concatenate([pick, pick], axis=1)
    for k in range(9):
        both = jnp.concatenate(two_parts(rows_grad[k]), axis=0)
        value = jnp.dot(pick2, both, preferred_element_type=F32)
        high = value.astype(BF16).astype(F32)
        grad_table[k] = high
        grad_table[9 + k] = value - high

    high_ids = lax.broadcasted_iota(jnp.int32, (his, LANES), 0)
    grad_copies = {}
    for j in sorted(range(WIN), key=lambda j: -abs(reach(j, nh))):
        summed = jnp.zeros((2 * comps, LANES), F32)
        for s in range(caps):
            e = j * caps + s
            wide = []
            for c in range(3):
                mine = high_ids == (ids_ref[c, e : e + 1, :] >> 7)
                wide.append(
                    jnp.concatenate(
                        [
                            jnp.where(mine, grad_table[half + c * 3 + d, e : e + 1, :], 0.0)
                            for half in (0, 9)
                            for d in range(3)
                        ],
                        axis=0,
                    )
                )
            both = jnp.concatenate(wide, axis=1).astype(BF16)
            summed = summed + lax.dot_general(both, vert_hot[e], NT, preferred_element_type=F32)
        grad_out[j] = summed[0:comps] + summed[comps:]
        if j != BACK:
            grad_copies[j] = pltpu.make_async_remote_copy(
                src_ref=grad_out.at[j], dst_ref=grad_in.at[j], send_sem=grad_send.at[j],
                recv_sem=grad_recv.at[j], device_id=(at_vertex(reach(j, nh)), v),
                device_id_type=MESH,
            )
            grad_copies[j].start()
    gathered = grad_out[BACK]
    for j in window:
        grad_copies[j].wait_recv()
        gathered = gathered + grad_in[j]
    view_in[v, 0:comps, :] = gathered
    view_in[v, comps : comps + 8, :] = energy_ref[...]
    out_copies = view_copies(view_in, view_send, view_recv)
    for copy in out_copies:
        copy.start()
    wait_views(view_in, view_recv)
    total = view_in[0]
    for other in range(1, nv):
        total = total + view_in[other]
    for d in range(3):
        for i in range(his):
            vgrad_ref[d : d + 1, i * LANES : (i + 1) * LANES] = total[
                d * his + i : d * his + i + 1, :
            ]

    share = jnp.zeros((2, nk), F32)
    for d in range(3):
        whole = vgrad_ref[d : d + 1, :]
        high = whole.astype(BF16).astype(F32)
        both = jnp.concatenate([high, whole - high], axis=0).astype(BF16)
        share = share + lax.dot_general(both, basis_v[d], NT, preferred_element_type=F32)
    share = share[0:1] + share[1:2]
    wide = min(nk, LANES)
    rows = nk // wide
    coeff_in[u] = jnp.zeros((8, LANES), F32)
    for i in range(rows):
        coeff_in[u, i : i + 1, 0:wide] = share[:, i * wide : (i + 1) * wide]
    coeff_in[u, rows : rows + 1, :] = jnp.sum(total[comps : comps + 8], axis=0, keepdims=True)
    coeff_copies = []
    for r in range(1, nh):
        coeff_copies.append(
            pltpu.make_async_remote_copy(
                src_ref=coeff_in.at[u], dst_ref=coeff_in.at[u], send_sem=coeff_send.at[r],
                recv_sem=coeff_recv.at[u], device_id=(at_vertex(r), v), device_id_type=MESH,
            )
        )
        coeff_copies[-1].start()

    for copies in (tri_copies, pos_copies, grad_copies):
        for j in window:
            copies[j].wait_send()
    for copy in part_copies + out_copies:
        copy.wait_send()
    for r in range(1, nh):
        other = at_vertex(r)
        pltpu.make_async_remote_copy(
            src_ref=coeff_in.at[other], dst_ref=coeff_in.at[other], send_sem=coeff_recv.at[other],
            recv_sem=coeff_recv.at[other], device_id=(other, v), device_id_type=MESH,
        ).wait_recv()
    total = coeff_in[0]
    for other in range(1, nh):
        total = total + coeff_in[other]
    for i in range(rows):
        coeff_ref[:, i * wide : (i + 1) * wide] = total[i : i + 1, 0:wide]
    loss_ref[...] = jnp.sum(total[rows : rows + 1, :], axis=1, keepdims=True) / pixel_total
    for copy in coeff_copies:
        copy.wait_send()


def per_device(
    nh, nv, coeffs, shape_basis, rest_pose, triangles, fetch_list, tile_cover, pix_slot,
    barycentric, camera, target,
):
    nk, _, verts = shape_basis.shape
    tiles, pix = pix_slot.shape
    covers = tile_cover.shape[1]
    caps = fetch_list.shape[2]
    live = WIN * caps
    comps = 3 * verts // LANES
    vmem = pl.BlockSpec(memory_space=pltpu.VMEM)
    hbm = pl.BlockSpec(memory_space=pl.ANY)
    dma = pltpu.SemaphoreType.DMA
    loss, vertex_grad, coeff_grad = pl.pallas_call(
        functools.partial(kernel, nh, nv, float(tiles * pix * nh * nv)),
        out_shape=(
            jax.ShapeDtypeStruct((1, 1), F32),
            jax.ShapeDtypeStruct((3, verts), F32),
            jax.ShapeDtypeStruct((1, nk), F32),
        ),
        in_specs=[hbm] * 10,
        out_specs=(vmem, vmem, vmem),
        scratch_shapes=[
            pltpu.VMEM((nk,), BF16),
            pltpu.VMEM((3, nk, verts), BF16),
            pltpu.VMEM((3, verts), F32),
            pltpu.SMEM((caps, nh), jnp.int32),
            pltpu.VMEM((covers, tiles), jnp.int32),
            pltpu.VMEM((tiles, pix), jnp.int32),
            pltpu.VMEM((3, tiles, pix), F32),
            pltpu.VMEM((12, tiles), F32),
            pltpu.VMEM((3, tiles, pix), F32),
            pltpu.VMEM((tiles, BLOCK, pix), BF16),
            pltpu.VMEM((live, LANES, 3 * LANES), BF16),
            pltpu.VMEM((nv, comps, LANES), F32),
            pltpu.VMEM((comps, LANES), F32),
            pltpu.VMEM((WIN, comps, LANES), F32),
            pltpu.VMEM((WIN,) + triangles.shape, jnp.int32),
            pltpu.VMEM((3, live, LANES), jnp.int32),
            pltpu.VMEM((live, 9 * LANES), F32),
            pltpu.VMEM((1, covers * tiles), jnp.int32),
            pltpu.VMEM((covers * tiles, 9 * LANES), F32),
            pltpu.VMEM((tiles, 12), F32),
            pltpu.VMEM((18, tiles, pix), F32),
            pltpu.VMEM((9, covers * tiles, LANES), F32),
            pltpu.VMEM((8, LANES), F32),
            pltpu.VMEM((18, live, LANES), F32),
            pltpu.VMEM((WIN, comps, LANES), F32),
            pltpu.VMEM((WIN, comps, LANES), F32),
            pltpu.VMEM((nv, comps + 8, LANES), F32),
            pltpu.VMEM((nh, 8, LANES), F32),
            dma((12,)),
            dma((WIN,)), dma((WIN,)),
            dma((nv,)), dma((nv,)),
            dma((WIN,)), dma((WIN,)),
            dma((WIN,)), dma((WIN,)),
            dma((nv,)), dma((nv,)),
            dma((nh,)), dma((nh,)),
        ],
        compiler_params=pltpu.CompilerParams(
            collective_id=0, has_side_effects=True, vmem_limit_bytes=62 * 1024 * 1024
        ),
    )(
        coeffs,
        jnp.transpose(shape_basis, (1, 0, 2)),
        rest_pose,
        triangles,
        jnp.transpose(fetch_list[0], (1, 0)),
        jnp.transpose(tile_cover, (1, 0)),
        pix_slot,
        jnp.transpose(barycentric, (1, 0, 2)),
        jnp.transpose(camera, (1, 0)),
        jnp.transpose(target, (1, 0, 2)),
    )
    return loss.reshape(()), vertex_grad, coeff_grad.reshape(nk)


def solution(mesh):
    placed = (
        P("view"),
        P("view", None, "vertex"),
        P(None, "vertex"),
        P(None, "vertex"),
        P(("vertex", "view"), None, None),
        P(("vertex", "view"), None),
        P(("vertex", "view"), None),
        P(("vertex", "view"), None, None),
        P(("vertex", "view"), None),
        P(("vertex", "view"), None, None),
    )
    return jax.shard_map(
        functools.partial(per_device, mesh.shape["vertex"], mesh.shape["view"]),
        mesh=mesh,
        in_specs=placed,
        out_specs=(P(), P(None, "vertex"), P("view")),
        check_vma=False,
    )
```

```python
import functools

import jax
import jax.numpy as jnp
from jax import lax
from jax.experimental import pallas as pl
from jax.experimental.pallas import tpu as pltpu
from jax.sharding import PartitionSpec as P

MESH = pl.DeviceIdType.MESH
BLOCK = 128
LANES = 128
WIN = 8
BACK = 3
SMOOTH = 0.1
F32 = jnp.float32
BF16 = jnp.bfloat16
NT = (((1,), (1,)), ((), ()))
TN = (((0,), (0,)), ((), ()))


def reach(j, holders):
    return holders // 2 if j == WIN - 1 else j - BACK


def pick_lanes(table, lanes):
    return jnp.take_along_axis(table, lanes, axis=1, mode="promise_in_bounds")


def two_parts(values):
    high = values.astype(BF16)
    low = (values - high.astype(F32)).astype(BF16)
    return high, low


def three_parts(values):
    high = values.astype(BF16)
    rest = values - high.astype(F32)
    middle = rest.astype(BF16)
    low = (rest - middle.astype(F32)).astype(BF16)
    return high, middle, low


def kernel(
    nh, nv,
    coeffs_in, basis_in, rest_in, tri_ref, fetch_in, cover_in, slot_in, bary_in, cam_in, target_in,
    vgrad_ref, sums_ref,
    coeffs_ref, basis_v, rest_ref, fetch_ref, cover_ref, slot_ref, bary_ref, cam_ref, target_ref,
    tile_hot, vert_hot, part, rest_rows, pos_all, tri_all, ids_ref, table, cover_row, rows_ref, cam_t,
    corner_grad, rows_grad, energy_ref, grad_table, grad_out, grad_in, view_in, energy_in,
    coeff_in,
    load_sem, tri_send, tri_recv, part_send, part_recv, pos_send, pos_recv, grad_send, grad_recv,
    view_send, view_recv, energy_send, energy_recv, coeff_send, coeff_recv,
):
    u = lax.axis_index("vertex")
    v = lax.axis_index("view")
    nk = basis_v.shape[1]
    his = rest_ref.shape[1] // LANES
    comps = 3 * his
    tiles = slot_ref.shape[0]
    pix = slot_ref.shape[1]
    covers = cover_ref.shape[0]
    caps = fetch_ref.shape[0]
    cap_bits = caps.bit_length() - 1
    live = WIN * caps
    window = [j for j in range(WIN) if j != BACK]

    def at_vertex(step):
        return lax.rem(u + step + nh, nh)

    def at_view(step):
        return lax.rem(v + step, nv)

    pairs = [
        (coeffs_in, coeffs_ref), (basis_in.at[0], basis_v.at[0]), (basis_in.at[1], basis_v.at[1]),
        (basis_in.at[2], basis_v.at[2]), (rest_in, rest_ref), (cover_in, cover_ref),
        (cam_in, cam_ref), (slot_in, slot_ref), (fetch_in, fetch_ref), (tri_ref, tri_all.at[BACK]),
        (bary_in, bary_ref), (target_in, target_ref),
    ]
    loads = [
        pltpu.make_async_copy(src, dst, load_sem.at[i]) for i, (src, dst) in enumerate(pairs)
    ]
    for load in loads[:4]:
        load.start()

    barrier = pltpu.get_barrier_semaphore()
    for r in range(1, nv):
        pl.semaphore_signal(barrier, inc=1, device_id=(u, at_view(r)), device_id_type=MESH)
    for r in range(1, nh):
        pl.semaphore_signal(barrier, inc=1, device_id=(at_vertex(r), v), device_id_type=MESH)
    for load in loads[4:]:
        load.start()

    loads[0].wait()
    for d in range(3):
        loads[1 + d].wait()
        share = jnp.dot(coeffs_ref[...].reshape(1, nk), basis_v[d], preferred_element_type=F32)
        for i in range(his):
            part[v, pl.ds(d * his + i, 1), :] = share[:, i * LANES : (i + 1) * LANES]

    pl.semaphore_wait(barrier, nh + nv - 2)

    def view_copies(buffer, send, recv):
        out = []
        for r in range(1, nv):
            out.append(
                pltpu.make_async_remote_copy(
                    src_ref=buffer.at[v], dst_ref=buffer.at[v], send_sem=send.at[r],
                    recv_sem=recv.at[v], device_id=(u, at_view(r)), device_id_type=MESH,
                )
            )
        return out

    def wait_views(buffer, recv):
        for r in range(1, nv):
            other = at_view(r)
            pltpu.make_async_remote_copy(
                src_ref=buffer.at[other], dst_ref=buffer.at[other], send_sem=recv.at[other],
                recv_sem=recv.at[other], device_id=(u, other), device_id_type=MESH,
            ).wait_recv()

    part_copies = view_copies(part, part_send, part_recv)
    for copy in part_copies:
        copy.start()
    tri_copies = {}
    for j in window:
        tri_copies[j] = pltpu.make_async_remote_copy(
            src_ref=tri_ref, dst_ref=tri_all.at[j], send_sem=tri_send.at[j],
            recv_sem=tri_recv.at[j], device_id=(at_vertex(-reach(j, nh)), v), device_id_type=MESH,
        )
        tri_copies[j].start()

    for load in loads[4:8]:
        load.wait()
    for d in range(3):
        for i in range(his):
            rest_rows[d * his + i : d * his + i + 1, :] = rest_ref[
                d : d + 1, i * LANES : (i + 1) * LANES
            ]
    entry = cover_ref[...]
    holder = entry >> cap_bits
    away = holder - u
    away = jnp.where(away < 0, away + nh, away)
    near = jnp.where(away <= BACK, away + BACK, away + BACK - nh)
    compact = jnp.where(away == nh // 2, WIN - 1, near) * caps + (entry & (caps - 1))
    for n in range(covers):
        cover_row[0:1, n * tiles : (n + 1) * tiles] = compact[n : n + 1, :]
    entry_ids = lax.broadcasted_iota(jnp.int32, (live, covers * tiles), 0)
    pick = (entry_ids == cover_row[...]).astype(F32).astype(BF16)
    cam_t[...] = jnp.transpose(cam_ref[...])

    lane_ids = lax.broadcasted_iota(jnp.int32, (BLOCK, pix), 0)

    def tile_lanes(t, carry):
        lanes = slot_ref[pl.ds(t, 1), :] & (BLOCK - 1)
        tile_hot[t] = (lane_ids == lanes).astype(F32).astype(BF16)
        return carry

    wait_views(part, part_recv)
    total = part[0]
    for other in range(1, nv):
        total = total + part[other]
    pos_all[BACK] = rest_rows[...] + total
    pos_copies = {}
    for j in window:
        pos_copies[j] = pltpu.make_async_remote_copy(
            src_ref=pos_all.at[BACK], dst_ref=pos_all.at[j], send_sem=pos_send.at[j],
            recv_sem=pos_recv.at[j], device_id=(at_vertex(-reach(j, nh)), v), device_id_type=MESH,
        )
        pos_copies[j].start()

    lax.fori_loop(0, tiles, tile_lanes, 0, unroll=4)
    loads[8].wait()
    loads[9].wait()
    for j in window:
        tri_copies[j].wait_recv()
    blocks = tri_ref.shape[1] // BLOCK
    for j in range(WIN):
        wanted = [
            jnp.full((3, BLOCK), fetch_ref[s, at_vertex(reach(j, nh))], jnp.int32)
            for s in range(caps)
        ]
        found = [jnp.zeros((3, BLOCK), jnp.int32)] * caps
        for b in range(blocks):
            corners = tri_all[j, :, b * BLOCK : (b + 1) * BLOCK]
            for s in range(caps):
                found[s] = jnp.where(wanted[s] == b, corners, found[s])
        for s in range(caps):
            for c in range(3):
                ids_ref[c, j * caps + s : j * caps + s + 1, :] = found[s][c : c + 1, :]

    low_ids = lax.broadcasted_iota(jnp.int32, (LANES, LANES), 0)

    def vertex_lanes(e, carry):
        for c in range(3):
            lows = ids_ref[c, pl.ds(e, 1), :] & (LANES - 1)
            vert_hot[e, :, c * LANES : (c + 1) * LANES] = (
                (low_ids == lows).astype(F32).astype(BF16)
            )
        return carry

    lax.fori_loop(0, live, vertex_lanes, 0, unroll=2)

    for j in window:
        pos_copies[j].wait_recv()

    sub8 = lax.broadcasted_iota(jnp.int32, (8, LANES), 0)
    shards = 8 // caps
    for q in range(live // 8):
        ids = [ids_ref[c, 8 * q : 8 * q + 8, :] for c in range(3)]
        lows = [x & (LANES - 1) for x in ids]
        highs = [x >> 7 for x in ids]
        sources = []
        for row in range(comps):
            source = None
            for w in range(shards):
                wide = jnp.broadcast_to(pos_all[q * shards + w, row : row + 1, :], (8, LANES))
                source = wide if source is None else jnp.where(sub8 >= w * caps, wide, source)
            sources.append(source)
        for c in range(3):
            masks = [highs[c] == i for i in range(his)]
            for d in range(3):
                picked = jnp.zeros((8, LANES), F32)
                for i in range(his):
                    picked = jnp.where(masks[i], pick_lanes(sources[d * his + i], lows[c]), picked)
                k = c * 3 + d
                table[8 * q : 8 * q + 8, k * LANES : (k + 1) * LANES] = picked

    pick3 = jnp.concatenate([pick, pick, pick], axis=0)
    parts = jnp.concatenate(three_parts(table[...]), axis=0)
    rows_ref[...] = lax.dot_general(pick3, parts, TN, preferred_element_type=F32)

    energy_ref[...] = jnp.zeros((8, LANES), F32)
    loads[10].wait()
    loads[11].wait()

    def shade(g, carry):
        base = pl.multiple_of(g * 8, 8)
        lens = [cam_t[pl.ds(base, 8), i : i + 1] for i in range(12)]
        for half in range(pix // LANES):
            span = slice(half * LANES, (half + 1) * LANES)
            slots = slot_ref[pl.ds(base, 8), span]
            lanes = slots & (BLOCK - 1)
            where_n = slots >> 7
            masks = [where_n == n for n in range(covers)]
            corners = []
            for k in range(9):
                picked = jnp.zeros((8, LANES), F32)
                for n in range(covers):
                    source = rows_ref[
                        pl.ds(pl.multiple_of(n * tiles + base, 8), 8), k * LANES : (k + 1) * LANES
                    ]
                    picked = jnp.where(masks[n], pick_lanes(source, lanes), picked)
                corners.append(picked)
            weights = [bary_ref[c, pl.ds(base, 8), span] for c in range(3)]
            surface = []
            for d in range(3):
                point = weights[0] * corners[d]
                point = point + weights[1] * corners[3 + d]
                surface.append(point + weights[2] * corners[6 + d])
            energy = energy_ref[...]
            grads = []
            for r in range(3):
                linear = lens[3 * r] * surface[0]
                linear = linear + lens[3 * r + 1] * surface[1]
                linear = linear + lens[3 * r + 2] * surface[2]
                shaded = jnp.tanh(linear + lens[9 + r])
                differ = shaded - target_ref[r, pl.ds(base, 8), span]
                square = differ * differ + SMOOTH * SMOOTH
                inverse = lax.rsqrt(square)
                energy = energy + square * inverse
                grads.append(differ * inverse * (1.0 - shaded * shaded))
            energy_ref[...] = energy
            for d in range(3):
                pull = lens[d] * grads[0] + lens[3 + d] * grads[1] + lens[6 + d] * grads[2]
                for c in range(3):
                    value = weights[c] * pull
                    high = value.astype(BF16).astype(F32)
                    corner_grad[c * 3 + d, pl.ds(base, 8), span] = high
                    corner_grad[9 + c * 3 + d, pl.ds(base, 8), span] = value - high
        return carry

    lax.fori_loop(0, tiles // 8, shade, 0)
    energy_in[v] = energy_ref[...]
    energy_copies = view_copies(energy_in, energy_send, energy_recv)
    for copy in energy_copies:
        copy.start()

    cover_ids = lax.broadcasted_iota(jnp.int32, (covers, pix), 0)

    def spread_tile(t, carry):
        mine = cover_ids == (slot_ref[pl.ds(t, 1), :] >> 7)
        both = jnp.concatenate(
            [jnp.where(mine, corner_grad[k, pl.ds(t, 1), :], 0.0) for k in range(18)], axis=0
        ).astype(BF16)
        summed = lax.dot_general(both, tile_hot[t], NT, preferred_element_type=F32)
        summed = summed[0 : 9 * covers] + summed[9 * covers :]
        for k in range(9):
            rows_grad[k, pl.ds(t, covers, stride=tiles), :] = summed[k * covers : (k + 1) * covers]
        return carry

    lax.fori_loop(0, tiles, spread_tile, 0, unroll=4)

    pick2 = jnp.concatenate([pick, pick], axis=1)
    for k in range(9):
        both = jnp.concatenate(two_parts(rows_grad[k]), axis=0)
        value = jnp.dot(pick2, both, preferred_element_type=F32)
        high = value.astype(BF16).astype(F32)
        grad_table[k] = high
        grad_table[9 + k] = value - high

    high_ids = lax.broadcasted_iota(jnp.int32, (his, LANES), 0)

    def shard_grad(j):
        summed = jnp.zeros((2 * comps, LANES), F32)
        for s in range(caps):
            e = j * caps + s
            wide = []
            for c in range(3):
                mine = high_ids == (ids_ref[c, pl.ds(e, 1), :] >> 7)
                wide.append(
                    jnp.concatenate(
                        [
                            jnp.where(mine, grad_table[half + c * 3 + d, pl.ds(e, 1), :], 0.0)
                            for half in (0, 9)
                            for d in range(3)
                        ],
                        axis=0,
                    )
                )
            both = jnp.concatenate(wide, axis=1).astype(BF16)
            summed = summed + lax.dot_general(both, vert_hot[e], NT, preferred_element_type=F32)
        return summed[0:comps] + summed[comps:]

    turns = WIN // nv

    def other_copy(r, m):
        w = at_view(r)
        return pltpu.make_async_remote_copy(
            src_ref=grad_out.at[m * nv + w], dst_ref=view_in.at[v, m],
            send_sem=view_send.at[r, m], recv_sem=view_recv.at[v, m], device_id=(u, w),
            device_id_type=MESH,
        )

    def holder_copy(r, m):
        j = m * nv + v
        step = j - BACK + (j // (WIN - 1)) * (nh // 2 - (WIN - 1 - BACK))
        return pltpu.make_async_remote_copy(
            src_ref=grad_out.at[j], dst_ref=grad_in.at[j], send_sem=grad_send.at[r, m],
            recv_sem=grad_recv.at[j], device_id=(at_vertex(step), at_view(r)),
            device_id_type=MESH,
        )

    for r in range(1, nv):

        def for_other(m, carry, r=r):
            j = m * nv + at_view(r)
            grad_out[j] = shard_grad(j)
            other_copy(r, m).start()
            return carry

        lax.fori_loop(0, turns, for_other, 0)

    def for_own(m, carry):
        j = m * nv + v
        total = shard_grad(j)
        for r in range(1, nv):
            w = at_view(r)
            pltpu.make_async_remote_copy(
                src_ref=view_in.at[w, m], dst_ref=view_in.at[w, m], send_sem=view_recv.at[w, m],
                recv_sem=view_recv.at[w, m], device_id=(u, w), device_id_type=MESH,
            ).wait_recv()
            total = total + view_in[w, m]
        grad_out[j] = total
        for r in range(1, nv):
            holder_copy(r, m).start()

        @pl.when(j != BACK)
        def _():
            holder_copy(0, m).start()

        @pl.when(j == BACK)
        def _():
            grad_in[BACK] = grad_out[BACK]

        return carry

    lax.fori_loop(0, turns, for_own, 0)

    def arrive(j):
        pltpu.make_async_remote_copy(
            src_ref=grad_in.at[j], dst_ref=grad_in.at[j], send_sem=grad_recv.at[j],
            recv_sem=grad_recv.at[j], device_id=(at_vertex(1), v), device_id_type=MESH,
        ).wait_recv()

    @pl.when(v != BACK % nv)
    def _():
        arrive(BACK)

    for j in window:
        arrive(j)
    total = grad_in[0]
    for j in range(1, WIN):
        total = total + grad_in[j]
    for d in range(3):
        for i in range(his):
            vgrad_ref[d : d + 1, i * LANES : (i + 1) * LANES] = total[
                d * his + i : d * his + i + 1, :
            ]

    share = jnp.zeros((2, nk), F32)
    for d in range(3):
        whole = vgrad_ref[d : d + 1, :]
        high = whole.astype(BF16).astype(F32)
        both = jnp.concatenate([high, whole - high], axis=0).astype(BF16)
        share = share + lax.dot_general(both, basis_v[d], NT, preferred_element_type=F32)
    share = share[0:1] + share[1:2]
    wide = min(nk, LANES)
    rows = nk // wide
    coeff_in[u] = jnp.zeros((8, LANES), F32)
    for i in range(rows):
        coeff_in[u, i : i + 1, 0:wide] = share[:, i * wide : (i + 1) * wide]
    wait_views(energy_in, energy_recv)
    energy = energy_in[0]
    for other in range(1, nv):
        energy = energy + energy_in[other]
    coeff_in[u, rows : rows + 1, :] = jnp.sum(energy, axis=0, keepdims=True)
    coeff_copies = []
    for r in range(1, nh):
        coeff_copies.append(
            pltpu.make_async_remote_copy(
                src_ref=coeff_in.at[u], dst_ref=coeff_in.at[u], send_sem=coeff_send.at[r],
                recv_sem=coeff_recv.at[u], device_id=(at_vertex(r), v), device_id_type=MESH,
            )
        )
        coeff_copies[-1].start()

    for copies in (tri_copies, pos_copies):
        for j in window:
            copies[j].wait_send()
    for copy in part_copies + energy_copies:
        copy.wait_send()

    def sent(m, carry):
        for r in range(1, nv):
            other_copy(r, m).wait_send()
            holder_copy(r, m).wait_send()

        @pl.when(m * nv + v != BACK)
        def _():
            holder_copy(0, m).wait_send()

        return carry

    lax.fori_loop(0, turns, sent, 0)
    for r in range(1, nh):
        other = at_vertex(r)
        pltpu.make_async_remote_copy(
            src_ref=coeff_in.at[other], dst_ref=coeff_in.at[other], send_sem=coeff_recv.at[other],
            recv_sem=coeff_recv.at[other], device_id=(other, v), device_id_type=MESH,
        ).wait_recv()
    total = coeff_in[0]
    for other in range(1, nh):
        total = total + coeff_in[other]
    sums_ref[...] = total
    for copy in coeff_copies:
        copy.wait_send()


def finish(pixel_total, gathered_ref, sums_ref, loss_ref, vgrad_ref, coeff_ref, sem):
    nk = coeff_ref.shape[1]
    wide = min(nk, LANES)
    rows = nk // wide
    copy = pltpu.make_async_copy(gathered_ref, vgrad_ref, sem)
    copy.start()
    for i in range(rows):
        coeff_ref[:, i * wide : (i + 1) * wide] = sums_ref[i : i + 1, 0:wide]
    energy = jnp.sum(sums_ref[rows : rows + 1, :], axis=1, keepdims=True)
    loss_ref[...] = energy / pixel_total
    copy.wait()


def per_device(
    nh, nv, coeffs, shape_basis, rest_pose, triangles, fetch_list, tile_cover, pix_slot,
    barycentric, camera, target,
):
    nk, _, verts = shape_basis.shape
    tiles, pix = pix_slot.shape
    covers = tile_cover.shape[1]
    caps = fetch_list.shape[2]
    live = WIN * caps
    comps = 3 * verts // LANES
    vmem = pl.BlockSpec(memory_space=pltpu.VMEM)
    hbm = pl.BlockSpec(memory_space=pl.ANY)
    dma = pltpu.SemaphoreType.DMA
    gathered, sums = pl.pallas_call(
        functools.partial(kernel, nh, nv),
        out_shape=(
            jax.ShapeDtypeStruct((3, verts), F32),
            jax.ShapeDtypeStruct((8, LANES), F32),
        ),
        in_specs=[hbm] * 10,
        out_specs=(vmem, vmem),
        scratch_shapes=[
            pltpu.VMEM((nk,), BF16),
            pltpu.VMEM((3, nk, verts), BF16),
            pltpu.VMEM((3, verts), F32),
            pltpu.SMEM((caps, nh), jnp.int32),
            pltpu.VMEM((covers, tiles), jnp.int32),
            pltpu.VMEM((tiles, pix), jnp.int32),
            pltpu.VMEM((3, tiles, pix), F32),
            pltpu.VMEM((12, tiles), F32),
            pltpu.VMEM((3, tiles, pix), F32),
            pltpu.VMEM((tiles, BLOCK, pix), BF16),
            pltpu.VMEM((live, LANES, 3 * LANES), BF16),
            pltpu.VMEM((nv, comps, LANES), F32),
            pltpu.VMEM((comps, LANES), F32),
            pltpu.VMEM((WIN, comps, LANES), F32),
            pltpu.VMEM((WIN,) + triangles.shape, jnp.int32),
            pltpu.VMEM((3, live, LANES), jnp.int32),
            pltpu.VMEM((live, 9 * LANES), F32),
            pltpu.VMEM((1, covers * tiles), jnp.int32),
            pltpu.VMEM((covers * tiles, 9 * LANES), F32),
            pltpu.VMEM((tiles, 12), F32),
            pltpu.VMEM((18, tiles, pix), F32),
            pltpu.VMEM((9, covers * tiles, LANES), F32),
            pltpu.VMEM((8, LANES), F32),
            pltpu.VMEM((18, live, LANES), F32),
            pltpu.VMEM((WIN, comps, LANES), F32),
            pltpu.VMEM((WIN, comps, LANES), F32),
            pltpu.VMEM((nv, WIN // nv, comps, LANES), F32),
            pltpu.VMEM((nv, 8, LANES), F32),
            pltpu.VMEM((nh, 8, LANES), F32),
            dma((12,)),
            dma((WIN,)), dma((WIN,)),
            dma((nv,)), dma((nv,)),
            dma((WIN,)), dma((WIN,)),
            dma((nv, WIN // nv)), dma((WIN,)),
            dma((nv, WIN // nv)), dma((nv, WIN // nv)),
            dma((nv,)), dma((nv,)),
            dma((nh,)), dma((nh,)),
        ],
        compiler_params=pltpu.CompilerParams(
            collective_id=0, has_side_effects=True, vmem_limit_bytes=62 * 1024 * 1024
        ),
    )(
        coeffs,
        jnp.transpose(shape_basis, (1, 0, 2)),
        rest_pose,
        triangles,
        jnp.transpose(fetch_list[0], (1, 0)),
        jnp.transpose(tile_cover, (1, 0)),
        pix_slot,
        jnp.transpose(barycentric, (1, 0, 2)),
        jnp.transpose(camera, (1, 0)),
        jnp.transpose(target, (1, 0, 2)),
    )
    loss, vertex_grad, coeff_grad = pl.pallas_call(
        functools.partial(finish, float(tiles * pix * nh * nv)),
        out_shape=(
            jax.ShapeDtypeStruct((1, 1), F32),
            jax.ShapeDtypeStruct((3, verts), F32),
            jax.ShapeDtypeStruct((1, nk), F32),
        ),
        in_specs=[hbm, vmem],
        out_specs=(vmem, hbm, vmem),
        scratch_shapes=[dma],
        compiler_params=pltpu.CompilerParams(vmem_limit_bytes=62 * 1024 * 1024),
    )(gathered, sums)
    return loss.reshape(()), vertex_grad, coeff_grad.reshape(nk)


def solution(mesh):
    placed = (
        P("view"),
        P("view", None, "vertex"),
        P(None, "vertex"),
        P(None, "vertex"),
        P(("vertex", "view"), None, None),
        P(("vertex", "view"), None),
        P(("vertex", "view"), None),
        P(("vertex", "view"), None, None),
        P(("vertex", "view"), None),
        P(("vertex", "view"), None, None),
    )
    return jax.shard_map(
        functools.partial(per_device, mesh.shape["vertex"], mesh.shape["view"]),
        mesh=mesh,
        in_specs=placed,
        out_specs=(P(), P(None, "vertex"), P("view")),
        check_vma=False,
    )
```

```python
import functools

import jax
import jax.numpy as jnp
from jax import lax
from jax.experimental import pallas as pl
from jax.experimental.pallas import tpu as pltpu
from jax.sharding import PartitionSpec as P

MESH = pl.DeviceIdType.MESH
BLOCK = 128
LANES = 128
WIN = 8
BACK = 3
SMOOTH = 0.1
F32 = jnp.float32
BF16 = jnp.bfloat16
NT = (((1,), (1,)), ((), ()))
TN = (((0,), (0,)), ((), ()))


def reach(j, holders):
    return holders // 2 if j == WIN - 1 else j - BACK


def pick_lanes(table, lanes):
    return jnp.take_along_axis(table, lanes, axis=1, mode="promise_in_bounds")


def two_parts(values):
    high = values.astype(BF16)
    low = (values - high.astype(F32)).astype(BF16)
    return high, low


def three_parts(values):
    high = values.astype(BF16)
    rest = values - high.astype(F32)
    middle = rest.astype(BF16)
    low = (rest - middle.astype(F32)).astype(BF16)
    return high, middle, low


def kernel(
    nh, nv,
    coeffs_in, basis_in, rest_in, tri_ref, fetch_in, cover_in, slot_in, bary_in, cam_in, target_in,
    vgrad_ref, sums_ref,
    coeffs_ref, basis_v, rest_ref, fetch_ref, cover_ref, slot_ref, bary_ref, cam_ref, target_ref,
    tile_hot, vert_hot, part, rest_rows, pos_all, tri_all, ids_ref, table, cover_row, rows_ref, cam_t,
    corner_grad, rows_grad, energy_ref, grad_table, grad_out, grad_in, view_in, energy_in,
    coeff_in,
    load_sem, tri_send, tri_recv, part_send, part_recv, pos_send, pos_recv, grad_send, grad_recv,
    view_send, view_recv, energy_send, energy_recv, coeff_send, coeff_recv,
):
    u = lax.axis_index("vertex")
    v = lax.axis_index("view")
    nk = basis_v.shape[1]
    his = rest_ref.shape[1] // LANES
    comps = 3 * his
    tiles = slot_ref.shape[0]
    pix = slot_ref.shape[1]
    covers = cover_ref.shape[0]
    caps = fetch_ref.shape[0]
    cap_bits = caps.bit_length() - 1
    live = WIN * caps
    window = [j for j in range(WIN) if j != BACK]

    def at_vertex(step):
        return lax.rem(u + step + nh, nh)

    def at_view(step):
        return lax.rem(v + step, nv)

    pairs = [
        (coeffs_in, coeffs_ref), (basis_in.at[0], basis_v.at[0]), (basis_in.at[1], basis_v.at[1]),
        (basis_in.at[2], basis_v.at[2]), (rest_in, rest_ref), (cover_in, cover_ref),
        (cam_in, cam_ref), (slot_in, slot_ref), (fetch_in, fetch_ref), (tri_ref, tri_all.at[BACK]),
        (bary_in, bary_ref), (target_in, target_ref),
    ]
    loads = [
        pltpu.make_async_copy(src, dst, load_sem.at[i]) for i, (src, dst) in enumerate(pairs)
    ]
    barrier = pltpu.get_barrier_semaphore()
    for r in range(1, nv):
        pl.semaphore_signal(barrier, inc=1, device_id=(u, at_view(r)), device_id_type=MESH)
    for r in range(1, nh):
        pl.semaphore_signal(barrier, inc=1, device_id=(at_vertex(r), v), device_id_type=MESH)
    for load in loads:
        load.start()

    loads[0].wait()
    for d in range(3):
        loads[1 + d].wait()
        share = jnp.dot(coeffs_ref[...].reshape(1, nk), basis_v[d], preferred_element_type=F32)
        for i in range(his):
            part[v, pl.ds(d * his + i, 1), :] = share[:, i * LANES : (i + 1) * LANES]

    pl.semaphore_wait(barrier, nh + nv - 2)

    def view_copies(buffer, send, recv):
        out = []
        for r in range(1, nv):
            out.append(
                pltpu.make_async_remote_copy(
                    src_ref=buffer.at[v], dst_ref=buffer.at[v], send_sem=send.at[r],
                    recv_sem=recv.at[v], device_id=(u, at_view(r)), device_id_type=MESH,
                )
            )
        return out

    def wait_views(buffer, recv):
        for r in range(1, nv):
            other = at_view(r)
            pltpu.make_async_remote_copy(
                src_ref=buffer.at[other], dst_ref=buffer.at[other], send_sem=recv.at[other],
                recv_sem=recv.at[other], device_id=(u, other), device_id_type=MESH,
            ).wait_recv()

    part_copies = view_copies(part, part_send, part_recv)
    for copy in part_copies:
        copy.start()
    tri_copies = {}
    for j in window:
        tri_copies[j] = pltpu.make_async_remote_copy(
            src_ref=tri_ref, dst_ref=tri_all.at[j], send_sem=tri_send.at[j],
            recv_sem=tri_recv.at[j], device_id=(at_vertex(-reach(j, nh)), v), device_id_type=MESH,
        )
        tri_copies[j].start()

    for load in loads[4:8]:
        load.wait()
    for d in range(3):
        for i in range(his):
            rest_rows[d * his + i : d * his + i + 1, :] = rest_ref[
                d : d + 1, i * LANES : (i + 1) * LANES
            ]
    entry = cover_ref[...]
    holder = entry >> cap_bits
    away = holder - u
    away = jnp.where(away < 0, away + nh, away)
    near = jnp.where(away <= BACK, away + BACK, away + BACK - nh)
    compact = jnp.where(away == nh // 2, WIN - 1, near) * caps + (entry & (caps - 1))
    for n in range(covers):
        cover_row[0:1, n * tiles : (n + 1) * tiles] = compact[n : n + 1, :]
    entry_ids = lax.broadcasted_iota(jnp.int32, (live, covers * tiles), 0)
    pick = (entry_ids == cover_row[...]).astype(F32).astype(BF16)
    cam_t[...] = jnp.transpose(cam_ref[...])

    lane_ids = lax.broadcasted_iota(jnp.int32, (BLOCK, pix), 0)

    def tile_lanes(t, carry):
        lanes = slot_ref[pl.ds(t, 1), :] & (BLOCK - 1)
        tile_hot[t] = (lane_ids == lanes).astype(F32).astype(BF16)
        return carry

    wait_views(part, part_recv)
    total = part[0]
    for other in range(1, nv):
        total = total + part[other]
    pos_all[BACK] = rest_rows[...] + total
    pos_copies = {}
    for j in window:
        pos_copies[j] = pltpu.make_async_remote_copy(
            src_ref=pos_all.at[BACK], dst_ref=pos_all.at[j], send_sem=pos_send.at[j],
            recv_sem=pos_recv.at[j], device_id=(at_vertex(-reach(j, nh)), v), device_id_type=MESH,
        )
        pos_copies[j].start()

    lax.fori_loop(0, tiles, tile_lanes, 0, unroll=4)
    loads[8].wait()
    loads[9].wait()
    for j in window:
        tri_copies[j].wait_recv()
    blocks = tri_ref.shape[1] // BLOCK
    for j in range(WIN):
        wanted = [
            jnp.full((3, BLOCK), fetch_ref[s, at_vertex(reach(j, nh))], jnp.int32)
            for s in range(caps)
        ]
        found = [jnp.zeros((3, BLOCK), jnp.int32)] * caps
        for b in range(blocks):
            corners = tri_all[j, :, b * BLOCK : (b + 1) * BLOCK]
            for s in range(caps):
                found[s] = jnp.where(wanted[s] == b, corners, found[s])
        for s in range(caps):
            for c in range(3):
                ids_ref[c, j * caps + s : j * caps + s + 1, :] = found[s][c : c + 1, :]

    low_ids = lax.broadcasted_iota(jnp.int32, (LANES, LANES), 0)

    def vertex_lanes(e, carry):
        for c in range(3):
            lows = ids_ref[c, pl.ds(e, 1), :] & (LANES - 1)
            vert_hot[e, :, c * LANES : (c + 1) * LANES] = (
                (low_ids == lows).astype(F32).astype(BF16)
            )
        return carry

    lax.fori_loop(0, live, vertex_lanes, 0, unroll=2)

    for j in window:
        pos_copies[j].wait_recv()

    sub8 = lax.broadcasted_iota(jnp.int32, (8, LANES), 0)
    shards = 8 // caps
    for q in range(live // 8):
        ids = [ids_ref[c, 8 * q : 8 * q + 8, :] for c in range(3)]
        lows = [x & (LANES - 1) for x in ids]
        highs = [x >> 7 for x in ids]
        sources = []
        for row in range(comps):
            source = None
            for w in range(shards):
                wide = jnp.broadcast_to(pos_all[q * shards + w, row : row + 1, :], (8, LANES))
                source = wide if source is None else jnp.where(sub8 >= w * caps, wide, source)
            sources.append(source)
        for c in range(3):
            masks = [highs[c] == i for i in range(his)]
            for d in range(3):
                picked = jnp.zeros((8, LANES), F32)
                for i in range(his):
                    picked = jnp.where(masks[i], pick_lanes(sources[d * his + i], lows[c]), picked)
                k = c * 3 + d
                table[8 * q : 8 * q + 8, k * LANES : (k + 1) * LANES] = picked

    pick3 = jnp.concatenate([pick, pick, pick], axis=0)
    parts = jnp.concatenate(three_parts(table[...]), axis=0)
    rows_ref[...] = lax.dot_general(pick3, parts, TN, preferred_element_type=F32)

    energy_ref[...] = jnp.zeros((8, LANES), F32)
    loads[10].wait()
    loads[11].wait()

    def shade(g):
        base = pl.multiple_of(g * 8, 8)
        lens = [cam_t[pl.ds(base, 8), i : i + 1] for i in range(12)]
        for half in range(pix // LANES):
            span = slice(half * LANES, (half + 1) * LANES)
            slots = slot_ref[pl.ds(base, 8), span]
            lanes = slots & (BLOCK - 1)
            where_n = slots >> 7
            masks = [where_n == n for n in range(covers)]
            corners = []
            for k in range(9):
                picked = jnp.zeros((8, LANES), F32)
                for n in range(covers):
                    source = rows_ref[
                        pl.ds(pl.multiple_of(n * tiles + base, 8), 8), k * LANES : (k + 1) * LANES
                    ]
                    picked = jnp.where(masks[n], pick_lanes(source, lanes), picked)
                corners.append(picked)
            weights = [bary_ref[c, pl.ds(base, 8), span] for c in range(3)]
            surface = []
            for d in range(3):
                point = weights[0] * corners[d]
                point = point + weights[1] * corners[3 + d]
                surface.append(point + weights[2] * corners[6 + d])
            energy = energy_ref[...]
            grads = []
            for r in range(3):
                linear = lens[3 * r] * surface[0]
                linear = linear + lens[3 * r + 1] * surface[1]
                linear = linear + lens[3 * r + 2] * surface[2]
                shaded = jnp.tanh(linear + lens[9 + r])
                differ = shaded - target_ref[r, pl.ds(base, 8), span]
                square = differ * differ + SMOOTH * SMOOTH
                inverse = lax.rsqrt(square)
                energy = energy + square * inverse
                grads.append(differ * inverse * (1.0 - shaded * shaded))
            energy_ref[...] = energy
            for d in range(3):
                pull = lens[d] * grads[0] + lens[3 + d] * grads[1] + lens[6 + d] * grads[2]
                for c in range(3):
                    value = weights[c] * pull
                    high = value.astype(BF16).astype(F32)
                    corner_grad[c * 3 + d, pl.ds(base, 8), span] = high
                    corner_grad[9 + c * 3 + d, pl.ds(base, 8), span] = value - high

    cover_ids = lax.broadcasted_iota(jnp.int32, (covers, pix), 0)

    def spread_tile(t):
        mine = cover_ids == (slot_ref[pl.ds(t, 1), :] >> 7)
        both = jnp.concatenate(
            [jnp.where(mine, corner_grad[k, pl.ds(t, 1), :], 0.0) for k in range(18)], axis=0
        ).astype(BF16)
        summed = lax.dot_general(both, tile_hot[t], NT, preferred_element_type=F32)
        summed = summed[0 : 9 * covers] + summed[9 * covers :]
        for k in range(9):
            rows_grad[k, pl.ds(t, covers, stride=tiles), :] = summed[k * covers : (k + 1) * covers]

    def spread_group(g):
        for i in range(8):
            spread_tile(g * 8 + i)

    groups = tiles // 8
    shade(0)

    def step(g, carry):
        spread_group(g - 1)
        shade(g)
        return carry

    lax.fori_loop(1, groups, step, 0)
    energy_in[v] = energy_ref[...]
    energy_copies = view_copies(energy_in, energy_send, energy_recv)
    for copy in energy_copies:
        copy.start()
    spread_group(groups - 1)

    pick2 = jnp.concatenate([pick, pick], axis=1)
    for k in range(9):
        both = jnp.concatenate(two_parts(rows_grad[k]), axis=0)
        value = jnp.dot(pick2, both, preferred_element_type=F32)
        high = value.astype(BF16).astype(F32)
        grad_table[k] = high
        grad_table[9 + k] = value - high

    high_ids = lax.broadcasted_iota(jnp.int32, (his, LANES), 0)

    def shard_grad(j):
        summed = jnp.zeros((2 * comps, LANES), F32)
        for s in range(caps):
            e = j * caps + s
            wide = []
            for c in range(3):
                mine = high_ids == (ids_ref[c, pl.ds(e, 1), :] >> 7)
                wide.append(
                    jnp.concatenate(
                        [
                            jnp.where(mine, grad_table[half + c * 3 + d, pl.ds(e, 1), :], 0.0)
                            for half in (0, 9)
                            for d in range(3)
                        ],
                        axis=0,
                    )
                )
            both = jnp.concatenate(wide, axis=1).astype(BF16)
            summed = summed + lax.dot_general(both, vert_hot[e], NT, preferred_element_type=F32)
        return summed[0:comps] + summed[comps:]

    turns = WIN // nv

    def other_copy(r, m):
        w = at_view(r)
        return pltpu.make_async_remote_copy(
            src_ref=grad_out.at[m * nv + w], dst_ref=view_in.at[v, m],
            send_sem=view_send.at[r, m], recv_sem=view_recv.at[v, m], device_id=(u, w),
            device_id_type=MESH,
        )

    def holder_copy(r, m):
        j = m * nv + v
        step = j - BACK + (j // (WIN - 1)) * (nh // 2 - (WIN - 1 - BACK))
        return pltpu.make_async_remote_copy(
            src_ref=grad_out.at[j], dst_ref=grad_in.at[j], send_sem=grad_send.at[r, m],
            recv_sem=grad_recv.at[j], device_id=(at_vertex(step), at_view(r)),
            device_id_type=MESH,
        )

    for r in range(1, nv):

        def for_other(m, carry, r=r):
            j = m * nv + at_view(r)
            grad_out[j] = shard_grad(j)
            other_copy(r, m).start()
            return carry

        lax.fori_loop(0, turns, for_other, 0)

    def for_own(m, carry):
        j = m * nv + v
        total = shard_grad(j)
        for r in range(1, nv):
            w = at_view(r)
            pltpu.make_async_remote_copy(
                src_ref=view_in.at[w, m], dst_ref=view_in.at[w, m], send_sem=view_recv.at[w, m],
                recv_sem=view_recv.at[w, m], device_id=(u, w), device_id_type=MESH,
            ).wait_recv()
            total = total + view_in[w, m]
        grad_out[j] = total
        for r in range(1, nv):
            holder_copy(r, m).start()

        @pl.when(j != BACK)
        def _():
            holder_copy(0, m).start()

        @pl.when(j == BACK)
        def _():
            grad_in[BACK] = grad_out[BACK]

        return carry

    lax.fori_loop(0, turns, for_own, 0)

    def arrive(j):
        pltpu.make_async_remote_copy(
            src_ref=grad_in.at[j], dst_ref=grad_in.at[j], send_sem=grad_recv.at[j],
            recv_sem=grad_recv.at[j], device_id=(at_vertex(1), v), device_id_type=MESH,
        ).wait_recv()

    @pl.when(v != BACK % nv)
    def _():
        arrive(BACK)

    for j in window:
        arrive(j)
    total = grad_in[0]
    for j in range(1, WIN):
        total = total + grad_in[j]
    for d in range(3):
        for i in range(his):
            vgrad_ref[d : d + 1, i * LANES : (i + 1) * LANES] = total[
                d * his + i : d * his + i + 1, :
            ]

    share = jnp.zeros((2, nk), F32)
    for d in range(3):
        whole = vgrad_ref[d : d + 1, :]
        high = whole.astype(BF16).astype(F32)
        both = jnp.concatenate([high, whole - high], axis=0).astype(BF16)
        share = share + lax.dot_general(both, basis_v[d], NT, preferred_element_type=F32)
    share = share[0:1] + share[1:2]
    wide = min(nk, LANES)
    rows = nk // wide
    coeff_in[u] = jnp.zeros((8, LANES), F32)
    for i in range(rows):
        coeff_in[u, i : i + 1, 0:wide] = share[:, i * wide : (i + 1) * wide]
    wait_views(energy_in, energy_recv)
    energy = energy_in[0]
    for other in range(1, nv):
        energy = energy + energy_in[other]
    coeff_in[u, rows : rows + 1, :] = jnp.sum(energy, axis=0, keepdims=True)
    coeff_copies = []
    for r in range(1, nh):
        coeff_copies.append(
            pltpu.make_async_remote_copy(
                src_ref=coeff_in.at[u], dst_ref=coeff_in.at[u], send_sem=coeff_send.at[r],
                recv_sem=coeff_recv.at[u], device_id=(at_vertex(r), v), device_id_type=MESH,
            )
        )
        coeff_copies[-1].start()

    for copies in (tri_copies, pos_copies):
        for j in window:
            copies[j].wait_send()
    for copy in part_copies + energy_copies:
        copy.wait_send()

    def sent(m, carry):
        for r in range(1, nv):
            other_copy(r, m).wait_send()
            holder_copy(r, m).wait_send()

        @pl.when(m * nv + v != BACK)
        def _():
            holder_copy(0, m).wait_send()

        return carry

    lax.fori_loop(0, turns, sent, 0)
    for r in range(1, nh):
        other = at_vertex(r)
        pltpu.make_async_remote_copy(
            src_ref=coeff_in.at[other], dst_ref=coeff_in.at[other], send_sem=coeff_recv.at[other],
            recv_sem=coeff_recv.at[other], device_id=(other, v), device_id_type=MESH,
        ).wait_recv()
    total = coeff_in[0]
    for other in range(1, nh):
        total = total + coeff_in[other]
    sums_ref[...] = total
    for copy in coeff_copies:
        copy.wait_send()


def finish(pixel_total, gathered_ref, sums_ref, loss_ref, vgrad_ref, coeff_ref):
    nk = coeff_ref.shape[1]
    wide = min(nk, LANES)
    rows = nk // wide
    vgrad_ref[...] = gathered_ref[...]
    for i in range(rows):
        coeff_ref[:, i * wide : (i + 1) * wide] = sums_ref[i : i + 1, 0:wide]
    energy = jnp.sum(sums_ref[rows : rows + 1, :], axis=1, keepdims=True)
    loss_ref[...] = energy / pixel_total


def per_device(
    nh, nv, coeffs, shape_basis, rest_pose, triangles, fetch_list, tile_cover, pix_slot,
    barycentric, camera, target,
):
    nk, _, verts = shape_basis.shape
    tiles, pix = pix_slot.shape
    covers = tile_cover.shape[1]
    caps = fetch_list.shape[2]
    live = WIN * caps
    comps = 3 * verts // LANES
    vmem = pl.BlockSpec(memory_space=pltpu.VMEM)
    hbm = pl.BlockSpec(memory_space=pl.ANY)
    dma = pltpu.SemaphoreType.DMA
    gathered, sums = pl.pallas_call(
        functools.partial(kernel, nh, nv),
        out_shape=(
            jax.ShapeDtypeStruct((3, verts), F32),
            jax.ShapeDtypeStruct((8, LANES), F32),
        ),
        in_specs=[hbm] * 10,
        out_specs=(vmem, vmem),
        scratch_shapes=[
            pltpu.VMEM((nk,), BF16),
            pltpu.VMEM((3, nk, verts), BF16),
            pltpu.VMEM((3, verts), F32),
            pltpu.SMEM((caps, nh), jnp.int32),
            pltpu.VMEM((covers, tiles), jnp.int32),
            pltpu.VMEM((tiles, pix), jnp.int32),
            pltpu.VMEM((3, tiles, pix), F32),
            pltpu.VMEM((12, tiles), F32),
            pltpu.VMEM((3, tiles, pix), F32),
            pltpu.VMEM((tiles, BLOCK, pix), BF16),
            pltpu.VMEM((live, LANES, 3 * LANES), BF16),
            pltpu.VMEM((nv, comps, LANES), F32),
            pltpu.VMEM((comps, LANES), F32),
            pltpu.VMEM((WIN, comps, LANES), F32),
            pltpu.VMEM((WIN,) + triangles.shape, jnp.int32),
            pltpu.VMEM((3, live, LANES), jnp.int32),
            pltpu.VMEM((live, 9 * LANES), F32),
            pltpu.VMEM((1, covers * tiles), jnp.int32),
            pltpu.VMEM((covers * tiles, 9 * LANES), F32),
            pltpu.VMEM((tiles, 12), F32),
            pltpu.VMEM((18, tiles, pix), F32),
            pltpu.VMEM((9, covers * tiles, LANES), F32),
            pltpu.VMEM((8, LANES), F32),
            pltpu.VMEM((18, live, LANES), F32),
            pltpu.VMEM((WIN, comps, LANES), F32),
            pltpu.VMEM((WIN, comps, LANES), F32),
            pltpu.VMEM((nv, WIN // nv, comps, LANES), F32),
            pltpu.VMEM((nv, 8, LANES), F32),
            pltpu.VMEM((nh, 8, LANES), F32),
            dma((12,)),
            dma((WIN,)), dma((WIN,)),
            dma((nv,)), dma((nv,)),
            dma((WIN,)), dma((WIN,)),
            dma((nv, WIN // nv)), dma((WIN,)),
            dma((nv, WIN // nv)), dma((nv, WIN // nv)),
            dma((nv,)), dma((nv,)),
            dma((nh,)), dma((nh,)),
        ],
        compiler_params=pltpu.CompilerParams(
            collective_id=0, has_side_effects=True, vmem_limit_bytes=62 * 1024 * 1024
        ),
    )(
        coeffs,
        jnp.transpose(shape_basis, (1, 0, 2)),
        rest_pose,
        triangles,
        jnp.transpose(fetch_list[0], (1, 0)),
        jnp.transpose(tile_cover, (1, 0)),
        pix_slot,
        jnp.transpose(barycentric, (1, 0, 2)),
        jnp.transpose(camera, (1, 0)),
        jnp.transpose(target, (1, 0, 2)),
    )
    loss, vertex_grad, coeff_grad = pl.pallas_call(
        functools.partial(finish, float(tiles * pix * nh * nv)),
        out_shape=(
            jax.ShapeDtypeStruct((1, 1), F32),
            jax.ShapeDtypeStruct((3, verts), F32),
            jax.ShapeDtypeStruct((1, nk), F32),
        ),
        in_specs=[vmem, vmem],
        out_specs=(vmem, vmem, vmem),
        compiler_params=pltpu.CompilerParams(vmem_limit_bytes=62 * 1024 * 1024),
    )(gathered, sums)
    return loss.reshape(()), vertex_grad, coeff_grad.reshape(nk)


def solution(mesh):
    placed = (
        P("view"),
        P("view", None, "vertex"),
        P(None, "vertex"),
        P(None, "vertex"),
        P(("vertex", "view"), None, None),
        P(("vertex", "view"), None),
        P(("vertex", "view"), None),
        P(("vertex", "view"), None, None),
        P(("vertex", "view"), None),
        P(("vertex", "view"), None, None),
    )
    return jax.shard_map(
        functools.partial(per_device, mesh.shape["vertex"], mesh.shape["view"]),
        mesh=mesh,
        in_specs=placed,
        out_specs=(P(), P(None, "vertex"), P("view")),
        check_vma=False,
    )
```

```python
import functools

import jax
import jax.numpy as jnp
from jax import lax
from jax.experimental import pallas as pl
from jax.experimental.pallas import tpu as pltpu
from jax.sharding import PartitionSpec as P

MESH = pl.DeviceIdType.MESH
BLOCK = 128
LANES = 128
WIN = 8
BACK = 3
SMOOTH = 0.1
F32 = jnp.float32
BF16 = jnp.bfloat16
NT = (((1,), (1,)), ((), ()))
TN = (((0,), (0,)), ((), ()))


def reach(j, holders):
    return holders // 2 if j == WIN - 1 else j - BACK


def pick_lanes(table, lanes):
    return jnp.take_along_axis(table, lanes, axis=1, mode="promise_in_bounds")


def two_parts(values):
    high = values.astype(BF16)
    low = (values - high.astype(F32)).astype(BF16)
    return high, low


def three_parts(values):
    high = values.astype(BF16)
    rest = values - high.astype(F32)
    middle = rest.astype(BF16)
    low = (rest - middle.astype(F32)).astype(BF16)
    return high, middle, low


def kernel(
    nh, nv,
    coeffs_in, basis_in, rest_in, tri_ref, fetch_in, cover_in, slot_in, bary_in, cam_in, target_in,
    vgrad_ref, sums_ref,
    coeffs_ref, basis_v, rest_ref, fetch_ref, cover_ref, slot_ref, bary_ref, cam_ref, target_ref,
    tile_hot, vert_hot, part, rest_rows, pos_all, tri_all, ids_ref, table, cover_row, rows_ref, cam_t,
    corner_grad, rows_grad, energy_ref, grad_table, grad_out, grad_in, view_in, energy_in,
    coeff_in,
    load_sem, tri_send, tri_recv, part_send, part_recv, pos_send, pos_recv, grad_send, grad_recv,
    view_send, view_recv, energy_send, energy_recv, coeff_send, coeff_recv,
):
    u = lax.axis_index("vertex")
    v = lax.axis_index("view")
    nk = basis_v.shape[1]
    his = rest_ref.shape[1] // LANES
    comps = 3 * his
    tiles = slot_ref.shape[0]
    pix = slot_ref.shape[1]
    covers = cover_ref.shape[0]
    caps = fetch_ref.shape[0]
    cap_bits = caps.bit_length() - 1
    live = WIN * caps
    window = [j for j in range(WIN) if j != BACK]

    def at_vertex(step):
        return lax.rem(u + step + nh, nh)

    def at_view(step):
        return lax.rem(v + step, nv)

    pairs = [
        (coeffs_in, coeffs_ref), (basis_in.at[0], basis_v.at[0]), (basis_in.at[1], basis_v.at[1]),
        (basis_in.at[2], basis_v.at[2]), (rest_in, rest_ref), (cover_in, cover_ref),
        (cam_in, cam_ref), (slot_in, slot_ref), (fetch_in, fetch_ref), (tri_ref, tri_all.at[BACK]),
        (bary_in, bary_ref), (target_in, target_ref),
    ]
    loads = [
        pltpu.make_async_copy(src, dst, load_sem.at[i]) for i, (src, dst) in enumerate(pairs)
    ]
    barrier = pltpu.get_barrier_semaphore()
    for r in range(1, nv):
        pl.semaphore_signal(barrier, inc=1, device_id=(u, at_view(r)), device_id_type=MESH)
    for r in range(1, nh):
        pl.semaphore_signal(barrier, inc=1, device_id=(at_vertex(r), v), device_id_type=MESH)
    for load in loads:
        load.start()

    loads[0].wait()
    for d in range(3):
        loads[1 + d].wait()
        share = jnp.dot(coeffs_ref[...].reshape(1, nk), basis_v[d], preferred_element_type=F32)
        for i in range(his):
            part[v, pl.ds(d * his + i, 1), :] = share[:, i * LANES : (i + 1) * LANES]

    pl.semaphore_wait(barrier, nh + nv - 2)

    def view_copies(buffer, send, recv):
        out = []
        for r in range(1, nv):
            out.append(
                pltpu.make_async_remote_copy(
                    src_ref=buffer.at[v], dst_ref=buffer.at[v], send_sem=send.at[r],
                    recv_sem=recv.at[v], device_id=(u, at_view(r)), device_id_type=MESH,
                )
            )
        return out

    def wait_views(buffer, recv):
        for r in range(1, nv):
            other = at_view(r)
            pltpu.make_async_remote_copy(
                src_ref=buffer.at[other], dst_ref=buffer.at[other], send_sem=recv.at[other],
                recv_sem=recv.at[other], device_id=(u, other), device_id_type=MESH,
            ).wait_recv()

    part_copies = view_copies(part, part_send, part_recv)
    for copy in part_copies:
        copy.start()
    tri_copies = {}
    for j in window:
        tri_copies[j] = pltpu.make_async_remote_copy(
            src_ref=tri_ref, dst_ref=tri_all.at[j], send_sem=tri_send.at[j],
            recv_sem=tri_recv.at[j], device_id=(at_vertex(-reach(j, nh)), v), device_id_type=MESH,
        )
        tri_copies[j].start()

    for load in loads[4:8]:
        load.wait()
    for d in range(3):
        for i in range(his):
            rest_rows[d * his + i : d * his + i + 1, :] = rest_ref[
                d : d + 1, i * LANES : (i + 1) * LANES
            ]
    entry = cover_ref[...]
    holder = entry >> cap_bits
    away = holder - u
    away = jnp.where(away < 0, away + nh, away)
    near = jnp.where(away <= BACK, away + BACK, away + BACK - nh)
    compact = jnp.where(away == nh // 2, WIN - 1, near) * caps + (entry & (caps - 1))
    for n in range(covers):
        cover_row[0:1, n * tiles : (n + 1) * tiles] = compact[n : n + 1, :]
    entry_ids = lax.broadcasted_iota(jnp.int32, (live, covers * tiles), 0)
    pick = (entry_ids == cover_row[...]).astype(F32).astype(BF16)
    cam_t[...] = jnp.transpose(cam_ref[...])

    lane_ids = lax.broadcasted_iota(jnp.int32, (BLOCK, pix), 0)

    def tile_lanes(t, carry):
        lanes = slot_ref[pl.ds(t, 1), :] & (BLOCK - 1)
        tile_hot[t] = jnp.transpose((lane_ids == lanes).astype(F32).astype(BF16))
        return carry

    wait_views(part, part_recv)
    total = part[0]
    for other in range(1, nv):
        total = total + part[other]
    pos_all[BACK] = rest_rows[...] + total
    pos_copies = {}
    for j in window:
        pos_copies[j] = pltpu.make_async_remote_copy(
            src_ref=pos_all.at[BACK], dst_ref=pos_all.at[j], send_sem=pos_send.at[j],
            recv_sem=pos_recv.at[j], device_id=(at_vertex(-reach(j, nh)), v), device_id_type=MESH,
        )
        pos_copies[j].start()

    lax.fori_loop(0, tiles, tile_lanes, 0, unroll=4)
    loads[8].wait()
    loads[9].wait()
    for j in window:
        tri_copies[j].wait_recv()
    blocks = tri_ref.shape[1] // BLOCK
    for j in range(WIN):
        wanted = [
            jnp.full((3, BLOCK), fetch_ref[s, at_vertex(reach(j, nh))], jnp.int32)
            for s in range(caps)
        ]
        found = [jnp.zeros((3, BLOCK), jnp.int32)] * caps
        for b in range(blocks):
            corners = tri_all[j, :, b * BLOCK : (b + 1) * BLOCK]
            for s in range(caps):
                found[s] = jnp.where(wanted[s] == b, corners, found[s])
        for s in range(caps):
            for c in range(3):
                ids_ref[c, j * caps + s : j * caps + s + 1, :] = found[s][c : c + 1, :]

    low_ids = lax.broadcasted_iota(jnp.int32, (LANES, LANES), 0)

    def vertex_lanes(e, carry):
        for c in range(3):
            lows = ids_ref[c, pl.ds(e, 1), :] & (LANES - 1)
            vert_hot[e, c * LANES : (c + 1) * LANES, :] = jnp.transpose(
                (low_ids == lows).astype(F32).astype(BF16)
            )
        return carry

    lax.fori_loop(0, live, vertex_lanes, 0, unroll=2)

    for j in window:
        pos_copies[j].wait_recv()

    sub8 = lax.broadcasted_iota(jnp.int32, (8, LANES), 0)
    shards = 8 // caps
    for q in range(live // 8):
        ids = [ids_ref[c, 8 * q : 8 * q + 8, :] for c in range(3)]
        lows = [x & (LANES - 1) for x in ids]
        highs = [x >> 7 for x in ids]
        sources = []
        for row in range(comps):
            source = None
            for w in range(shards):
                wide = jnp.broadcast_to(pos_all[q * shards + w, row : row + 1, :], (8, LANES))
                source = wide if source is None else jnp.where(sub8 >= w * caps, wide, source)
            sources.append(source)
        for c in range(3):
            masks = [highs[c] == i for i in range(his)]
            for d in range(3):
                picked = jnp.zeros((8, LANES), F32)
                for i in range(his):
                    picked = jnp.where(masks[i], pick_lanes(sources[d * his + i], lows[c]), picked)
                k = c * 3 + d
                table[8 * q : 8 * q + 8, k * LANES : (k + 1) * LANES] = picked

    pick3 = jnp.concatenate([pick, pick, pick], axis=0)
    parts = jnp.concatenate(three_parts(table[...]), axis=0)
    rows_ref[...] = lax.dot_general(pick3, parts, TN, preferred_element_type=F32)

    energy_ref[...] = jnp.zeros((8, LANES), F32)
    loads[10].wait()
    loads[11].wait()

    def shade(g):
        base = pl.multiple_of(g * 8, 8)
        lens = [cam_t[pl.ds(base, 8), i : i + 1] for i in range(12)]
        for half in range(pix // LANES):
            span = slice(half * LANES, (half + 1) * LANES)
            slots = slot_ref[pl.ds(base, 8), span]
            lanes = slots & (BLOCK - 1)
            where_n = slots >> 7
            masks = [where_n == n for n in range(covers)]
            corners = []
            for k in range(9):
                picked = jnp.zeros((8, LANES), F32)
                for n in range(covers):
                    source = rows_ref[
                        pl.ds(pl.multiple_of(n * tiles + base, 8), 8), k * LANES : (k + 1) * LANES
                    ]
                    picked = jnp.where(masks[n], pick_lanes(source, lanes), picked)
                corners.append(picked)
            weights = [bary_ref[c, pl.ds(base, 8), span] for c in range(3)]
            surface = []
            for d in range(3):
                point = weights[0] * corners[d]
                point = point + weights[1] * corners[3 + d]
                surface.append(point + weights[2] * corners[6 + d])
            energy = energy_ref[...]
            grads = []
            for r in range(3):
                linear = lens[3 * r] * surface[0]
                linear = linear + lens[3 * r + 1] * surface[1]
                linear = linear + lens[3 * r + 2] * surface[2]
                shaded = jnp.tanh(linear + lens[9 + r])
                differ = shaded - target_ref[r, pl.ds(base, 8), span]
                square = differ * differ + SMOOTH * SMOOTH
                inverse = lax.rsqrt(square)
                energy = energy + square * inverse
                grads.append(differ * inverse * (1.0 - shaded * shaded))
            energy_ref[...] = energy
            for d in range(3):
                pull = lens[d] * grads[0] + lens[3 + d] * grads[1] + lens[6 + d] * grads[2]
                for c in range(3):
                    value = weights[c] * pull
                    high = value.astype(BF16).astype(F32)
                    corner_grad[c * 3 + d, pl.ds(base, 8), span] = high
                    corner_grad[9 + c * 3 + d, pl.ds(base, 8), span] = value - high

    cover_ids = lax.broadcasted_iota(jnp.int32, (covers, pix), 0)

    def spread_tile(t):
        mine = cover_ids == (slot_ref[pl.ds(t, 1), :] >> 7)
        both = jnp.concatenate(
            [jnp.where(mine, corner_grad[k, pl.ds(t, 1), :], 0.0) for k in range(18)], axis=0
        ).astype(BF16)
        summed = jnp.dot(both, tile_hot[t], preferred_element_type=F32)
        summed = summed[0 : 9 * covers] + summed[9 * covers :]
        for k in range(9):
            rows_grad[k, pl.ds(t, covers, stride=tiles), :] = summed[k * covers : (k + 1) * covers]

    def spread_group(g):
        for i in range(8):
            spread_tile(g * 8 + i)

    groups = tiles // 8
    shade(0)

    def step(g, carry):
        spread_group(g - 1)
        shade(g)
        return carry

    lax.fori_loop(1, groups, step, 0)
    energy_in[v] = energy_ref[...]
    energy_copies = view_copies(energy_in, energy_send, energy_recv)
    for copy in energy_copies:
        copy.start()
    spread_group(groups - 1)

    pick2 = jnp.concatenate([pick, pick], axis=1)
    for k in range(9):
        both = jnp.concatenate(two_parts(rows_grad[k]), axis=0)
        value = jnp.dot(pick2, both, preferred_element_type=F32)
        high = value.astype(BF16).astype(F32)
        grad_table[k] = high
        grad_table[9 + k] = value - high

    high_ids = lax.broadcasted_iota(jnp.int32, (his, LANES), 0)

    def shard_grad(j):
        summed = jnp.zeros((2 * comps, LANES), F32)
        for s in range(caps):
            e = j * caps + s
            wide = []
            for c in range(3):
                mine = high_ids == (ids_ref[c, pl.ds(e, 1), :] >> 7)
                wide.append(
                    jnp.concatenate(
                        [
                            jnp.where(mine, grad_table[half + c * 3 + d, pl.ds(e, 1), :], 0.0)
                            for half in (0, 9)
                            for d in range(3)
                        ],
                        axis=0,
                    )
                )
            both = jnp.concatenate(wide, axis=1).astype(BF16)
            summed = summed + jnp.dot(both, vert_hot[e], preferred_element_type=F32)
        return summed[0:comps] + summed[comps:]

    turns = WIN // nv

    def other_copy(r, m):
        w = at_view(r)
        return pltpu.make_async_remote_copy(
            src_ref=grad_out.at[m * nv + w], dst_ref=view_in.at[v, m],
            send_sem=view_send.at[r, m], recv_sem=view_recv.at[v, m], device_id=(u, w),
            device_id_type=MESH,
        )

    def holder_copy(r, m):
        j = m * nv + v
        step = j - BACK + (j // (WIN - 1)) * (nh // 2 - (WIN - 1 - BACK))
        return pltpu.make_async_remote_copy(
            src_ref=grad_out.at[j], dst_ref=grad_in.at[j], send_sem=grad_send.at[r, m],
            recv_sem=grad_recv.at[j], device_id=(at_vertex(step), at_view(r)),
            device_id_type=MESH,
        )

    for r in range(1, nv):

        def for_other(m, carry, r=r):
            j = m * nv + at_view(r)
            grad_out[j] = shard_grad(j)
            other_copy(r, m).start()
            return carry

        lax.fori_loop(0, turns, for_other, 0)

    def for_own(m, carry):
        j = m * nv + v
        total = shard_grad(j)
        for r in range(1, nv):
            w = at_view(r)
            pltpu.make_async_remote_copy(
                src_ref=view_in.at[w, m], dst_ref=view_in.at[w, m], send_sem=view_recv.at[w, m],
                recv_sem=view_recv.at[w, m], device_id=(u, w), device_id_type=MESH,
            ).wait_recv()
            total = total + view_in[w, m]
        grad_out[j] = total
        for r in range(1, nv):
            holder_copy(r, m).start()

        @pl.when(j != BACK)
        def _():
            holder_copy(0, m).start()

        @pl.when(j == BACK)
        def _():
            grad_in[BACK] = grad_out[BACK]

        return carry

    lax.fori_loop(0, turns, for_own, 0)

    def arrive(j):
        pltpu.make_async_remote_copy(
            src_ref=grad_in.at[j], dst_ref=grad_in.at[j], send_sem=grad_recv.at[j],
            recv_sem=grad_recv.at[j], device_id=(at_vertex(1), v), device_id_type=MESH,
        ).wait_recv()

    @pl.when(v != BACK % nv)
    def _():
        arrive(BACK)

    for j in window:
        arrive(j)
    total = grad_in[0]
    for j in range(1, WIN):
        total = total + grad_in[j]
    for d in range(3):
        for i in range(his):
            vgrad_ref[d : d + 1, i * LANES : (i + 1) * LANES] = total[
                d * his + i : d * his + i + 1, :
            ]

    share = jnp.zeros((2, nk), F32)
    for d in range(3):
        whole = vgrad_ref[d : d + 1, :]
        high = whole.astype(BF16).astype(F32)
        both = jnp.concatenate([high, whole - high], axis=0).astype(BF16)
        share = share + lax.dot_general(both, basis_v[d], NT, preferred_element_type=F32)
    share = share[0:1] + share[1:2]
    wide = min(nk, LANES)
    rows = nk // wide
    coeff_in[u] = jnp.zeros((8, LANES), F32)
    for i in range(rows):
        coeff_in[u, i : i + 1, 0:wide] = share[:, i * wide : (i + 1) * wide]
    wait_views(energy_in, energy_recv)
    energy = energy_in[0]
    for other in range(1, nv):
        energy = energy + energy_in[other]
    coeff_in[u, rows : rows + 1, :] = jnp.sum(energy, axis=0, keepdims=True)
    coeff_copies = []
    for r in range(1, nh):
        coeff_copies.append(
            pltpu.make_async_remote_copy(
                src_ref=coeff_in.at[u], dst_ref=coeff_in.at[u], send_sem=coeff_send.at[r],
                recv_sem=coeff_recv.at[u], device_id=(at_vertex(r), v), device_id_type=MESH,
            )
        )
        coeff_copies[-1].start()

    for copies in (tri_copies, pos_copies):
        for j in window:
            copies[j].wait_send()
    for copy in part_copies + energy_copies:
        copy.wait_send()

    def sent(m, carry):
        for r in range(1, nv):
            other_copy(r, m).wait_send()
            holder_copy(r, m).wait_send()

        @pl.when(m * nv + v != BACK)
        def _():
            holder_copy(0, m).wait_send()

        return carry

    lax.fori_loop(0, turns, sent, 0)
    for r in range(1, nh):
        other = at_vertex(r)
        pltpu.make_async_remote_copy(
            src_ref=coeff_in.at[other], dst_ref=coeff_in.at[other], send_sem=coeff_recv.at[other],
            recv_sem=coeff_recv.at[other], device_id=(other, v), device_id_type=MESH,
        ).wait_recv()
    total = coeff_in[0]
    for other in range(1, nh):
        total = total + coeff_in[other]
    sums_ref[...] = total
    for copy in coeff_copies:
        copy.wait_send()


def finish(pixel_total, gathered_ref, sums_ref, loss_ref, vgrad_ref, coeff_ref):
    nk = coeff_ref.shape[1]
    wide = min(nk, LANES)
    rows = nk // wide
    vgrad_ref[...] = gathered_ref[...]
    for i in range(rows):
        coeff_ref[:, i * wide : (i + 1) * wide] = sums_ref[i : i + 1, 0:wide]
    energy = jnp.sum(sums_ref[rows : rows + 1, :], axis=1, keepdims=True)
    loss_ref[...] = energy / pixel_total


def per_device(
    nh, nv, coeffs, shape_basis, rest_pose, triangles, fetch_list, tile_cover, pix_slot,
    barycentric, camera, target,
):
    nk, _, verts = shape_basis.shape
    tiles, pix = pix_slot.shape
    covers = tile_cover.shape[1]
    caps = fetch_list.shape[2]
    live = WIN * caps
    comps = 3 * verts // LANES
    vmem = pl.BlockSpec(memory_space=pltpu.VMEM)
    hbm = pl.BlockSpec(memory_space=pl.ANY)
    dma = pltpu.SemaphoreType.DMA
    gathered, sums = pl.pallas_call(
        functools.partial(kernel, nh, nv),
        out_shape=(
            jax.ShapeDtypeStruct((3, verts), F32),
            jax.ShapeDtypeStruct((8, LANES), F32),
        ),
        in_specs=[hbm] * 10,
        out_specs=(vmem, vmem),
        scratch_shapes=[
            pltpu.VMEM((nk,), BF16),
            pltpu.VMEM((3, nk, verts), BF16),
            pltpu.VMEM((3, verts), F32),
            pltpu.SMEM((caps, nh), jnp.int32),
            pltpu.VMEM((covers, tiles), jnp.int32),
            pltpu.VMEM((tiles, pix), jnp.int32),
            pltpu.VMEM((3, tiles, pix), F32),
            pltpu.VMEM((12, tiles), F32),
            pltpu.VMEM((3, tiles, pix), F32),
            pltpu.VMEM((tiles, pix, BLOCK), BF16),
            pltpu.VMEM((live, 3 * LANES, LANES), BF16),
            pltpu.VMEM((nv, comps, LANES), F32),
            pltpu.VMEM((comps, LANES), F32),
            pltpu.VMEM((WIN, comps, LANES), F32),
            pltpu.VMEM((WIN,) + triangles.shape, jnp.int32),
            pltpu.VMEM((3, live, LANES), jnp.int32),
            pltpu.VMEM((live, 9 * LANES), F32),
            pltpu.VMEM((1, covers * tiles), jnp.int32),
            pltpu.VMEM((covers * tiles, 9 * LANES), F32),
            pltpu.VMEM((tiles, 12), F32),
            pltpu.VMEM((18, tiles, pix), F32),
            pltpu.VMEM((9, covers * tiles, LANES), F32),
            pltpu.VMEM((8, LANES), F32),
            pltpu.VMEM((18, live, LANES), F32),
            pltpu.VMEM((WIN, comps, LANES), F32),
            pltpu.VMEM((WIN, comps, LANES), F32),
            pltpu.VMEM((nv, WIN // nv, comps, LANES), F32),
            pltpu.VMEM((nv, 8, LANES), F32),
            pltpu.VMEM((nh, 8, LANES), F32),
            dma((12,)),
            dma((WIN,)), dma((WIN,)),
            dma((nv,)), dma((nv,)),
            dma((WIN,)), dma((WIN,)),
            dma((nv, WIN // nv)), dma((WIN,)),
            dma((nv, WIN // nv)), dma((nv, WIN // nv)),
            dma((nv,)), dma((nv,)),
            dma((nh,)), dma((nh,)),
        ],
        compiler_params=pltpu.CompilerParams(
            collective_id=0, has_side_effects=True, vmem_limit_bytes=62 * 1024 * 1024
        ),
    )(
        coeffs,
        jnp.transpose(shape_basis, (1, 0, 2)),
        rest_pose,
        triangles,
        jnp.transpose(fetch_list[0], (1, 0)),
        jnp.transpose(tile_cover, (1, 0)),
        pix_slot,
        jnp.transpose(barycentric, (1, 0, 2)),
        jnp.transpose(camera, (1, 0)),
        jnp.transpose(target, (1, 0, 2)),
    )
    loss, vertex_grad, coeff_grad = pl.pallas_call(
        functools.partial(finish, float(tiles * pix * nh * nv)),
        out_shape=(
            jax.ShapeDtypeStruct((1, 1), F32),
            jax.ShapeDtypeStruct((3, verts), F32),
            jax.ShapeDtypeStruct((1, nk), F32),
        ),
        in_specs=[vmem, vmem],
        out_specs=(vmem, vmem, vmem),
        compiler_params=pltpu.CompilerParams(vmem_limit_bytes=62 * 1024 * 1024),
    )(gathered, sums)
    return loss.reshape(()), vertex_grad, coeff_grad.reshape(nk)


def solution(mesh):
    placed = (
        P("view"),
        P("view", None, "vertex"),
        P(None, "vertex"),
        P(None, "vertex"),
        P(("vertex", "view"), None, None),
        P(("vertex", "view"), None),
        P(("vertex", "view"), None),
        P(("vertex", "view"), None, None),
        P(("vertex", "view"), None),
        P(("vertex", "view"), None, None),
    )
    return jax.shard_map(
        functools.partial(per_device, mesh.shape["vertex"], mesh.shape["view"]),
        mesh=mesh,
        in_specs=placed,
        out_specs=(P(), P(None, "vertex"), P("view")),
        check_vma=False,
    )
```

```python
import functools

import jax
import jax.numpy as jnp
from jax import lax
from jax.experimental import pallas as pl
from jax.experimental.pallas import tpu as pltpu
from jax.sharding import PartitionSpec as P

MESH = pl.DeviceIdType.MESH
BLOCK = 128
LANES = 128
WIN = 8
BACK = 3
SMOOTH = 0.1
F32 = jnp.float32
BF16 = jnp.bfloat16
NT = (((1,), (1,)), ((), ()))
TN = (((0,), (0,)), ((), ()))


def reach(j, holders):
    return holders // 2 if j == WIN - 1 else j - BACK


def pick_lanes(table, lanes):
    return jnp.take_along_axis(table, lanes, axis=1, mode="promise_in_bounds")


def two_parts(values):
    high = values.astype(BF16)
    low = (values - high.astype(F32)).astype(BF16)
    return high, low


def three_parts(values):
    high = values.astype(BF16)
    rest = values - high.astype(F32)
    middle = rest.astype(BF16)
    low = (rest - middle.astype(F32)).astype(BF16)
    return high, middle, low


def kernel(
    nh, nv,
    coeffs_in, basis_in, rest_in, tri_ref, fetch_in, cover_in, slot_in, bary_in, cam_in, target_in,
    vgrad_ref, sums_ref,
    coeffs_ref, basis_v, rest_ref, fetch_ref, cover_ref, slot_ref, bary_ref, cam_ref, target_ref,
    tile_hot, vert_hot, part, rest_rows, pos_all, tri_all, ids_ref, table, cover_row, rows_ref, cam_t,
    corner_grad, rows_grad, energy_ref, grad_table, grad_out, grad_in, view_in, energy_in,
    coeff_in,
    load_sem, tri_send, tri_recv, part_send, part_recv, pos_send, pos_recv, grad_send, grad_recv,
    view_send, view_recv, energy_send, energy_recv, coeff_send, coeff_recv,
):
    u = lax.axis_index("vertex")
    v = lax.axis_index("view")
    nk = basis_v.shape[1]
    his = rest_ref.shape[1] // LANES
    comps = 3 * his
    tiles = slot_ref.shape[0]
    pix = slot_ref.shape[1]
    covers = cover_ref.shape[0]
    caps = fetch_ref.shape[0]
    cap_bits = caps.bit_length() - 1
    live = WIN * caps
    window = [j for j in range(WIN) if j != BACK]

    def at_vertex(step):
        return lax.rem(u + step + nh, nh)

    def at_view(step):
        return lax.rem(v + step, nv)

    pairs = [
        (coeffs_in, coeffs_ref), (basis_in.at[0], basis_v.at[0]), (basis_in.at[1], basis_v.at[1]),
        (basis_in.at[2], basis_v.at[2]), (rest_in, rest_ref), (cover_in, cover_ref),
        (cam_in, cam_ref), (slot_in, slot_ref), (fetch_in, fetch_ref), (tri_ref, tri_all.at[BACK]),
        (bary_in, bary_ref), (target_in, target_ref),
    ]
    loads = [
        pltpu.make_async_copy(src, dst, load_sem.at[i]) for i, (src, dst) in enumerate(pairs)
    ]
    barrier = pltpu.get_barrier_semaphore()
    for r in range(1, nv):
        pl.semaphore_signal(barrier, inc=1, device_id=(u, at_view(r)), device_id_type=MESH)
    for r in sorted(range(1, nh), key=lambda r: abs(r - nh // 2)):
        pl.semaphore_signal(barrier, inc=1, device_id=(at_vertex(r), v), device_id_type=MESH)
    for load in loads:
        load.start()

    loads[0].wait()
    for d in range(3):
        loads[1 + d].wait()
        share = jnp.dot(coeffs_ref[...].reshape(1, nk), basis_v[d], preferred_element_type=F32)
        for i in range(his):
            part[v, pl.ds(d * his + i, 1), :] = share[:, i * LANES : (i + 1) * LANES]

    pl.semaphore_wait(barrier, nh + nv - 2)

    def view_copies(buffer, send, recv):
        out = []
        for r in range(1, nv):
            out.append(
                pltpu.make_async_remote_copy(
                    src_ref=buffer.at[v], dst_ref=buffer.at[v], send_sem=send.at[r],
                    recv_sem=recv.at[v], device_id=(u, at_view(r)), device_id_type=MESH,
                )
            )
        return out

    def wait_views(buffer, recv):
        for r in range(1, nv):
            other = at_view(r)
            pltpu.make_async_remote_copy(
                src_ref=buffer.at[other], dst_ref=buffer.at[other], send_sem=recv.at[other],
                recv_sem=recv.at[other], device_id=(u, other), device_id_type=MESH,
            ).wait_recv()

    part_copies = view_copies(part, part_send, part_recv)
    for copy in part_copies:
        copy.start()
    tri_copies = {}
    for j in window:
        tri_copies[j] = pltpu.make_async_remote_copy(
            src_ref=tri_ref, dst_ref=tri_all.at[j], send_sem=tri_send.at[j],
            recv_sem=tri_recv.at[j], device_id=(at_vertex(-reach(j, nh)), v), device_id_type=MESH,
        )
        tri_copies[j].start()

    for load in loads[4:8]:
        load.wait()
    for d in range(3):
        for i in range(his):
            rest_rows[d * his + i : d * his + i + 1, :] = rest_ref[
                d : d + 1, i * LANES : (i + 1) * LANES
            ]
    entry = cover_ref[...]
    holder = entry >> cap_bits
    away = holder - u
    away = jnp.where(away < 0, away + nh, away)
    near = jnp.where(away <= BACK, away + BACK, away + BACK - nh)
    compact = jnp.where(away == nh // 2, WIN - 1, near) * caps + (entry & (caps - 1))
    for n in range(covers):
        cover_row[0:1, n * tiles : (n + 1) * tiles] = compact[n : n + 1, :]
    entry_ids = lax.broadcasted_iota(jnp.int32, (live, covers * tiles), 0)
    pick = (entry_ids == cover_row[...]).astype(F32).astype(BF16)
    cam_t[...] = jnp.transpose(cam_ref[...])

    lane_ids = lax.broadcasted_iota(jnp.int32, (BLOCK, pix), 0)

    def tile_lanes(t, carry):
        lanes = slot_ref[pl.ds(t, 1), :] & (BLOCK - 1)
        tile_hot[t] = (lane_ids == lanes).astype(F32).astype(BF16)
        return carry

    wait_views(part, part_recv)
    total = part[0]
    for other in range(1, nv):
        total = total + part[other]
    pos_all[BACK] = rest_rows[...] + total
    pos_copies = {}
    for j in window:
        pos_copies[j] = pltpu.make_async_remote_copy(
            src_ref=pos_all.at[BACK], dst_ref=pos_all.at[j], send_sem=pos_send.at[j],
            recv_sem=pos_recv.at[j], device_id=(at_vertex(-reach(j, nh)), v), device_id_type=MESH,
        )
        pos_copies[j].start()

    lax.fori_loop(0, tiles, tile_lanes, 0, unroll=4)
    loads[8].wait()
    loads[9].wait()
    for j in window:
        tri_copies[j].wait_recv()
    blocks = tri_ref.shape[1] // BLOCK
    for j in range(WIN):
        wanted = [
            jnp.full((3, BLOCK), fetch_ref[s, at_vertex(reach(j, nh))], jnp.int32)
            for s in range(caps)
        ]
        found = [jnp.zeros((3, BLOCK), jnp.int32)] * caps
        for b in range(blocks):
            corners = tri_all[j, :, b * BLOCK : (b + 1) * BLOCK]
            for s in range(caps):
                found[s] = jnp.where(wanted[s] == b, corners, found[s])
        for s in range(caps):
            for c in range(3):
                ids_ref[c, j * caps + s : j * caps + s + 1, :] = found[s][c : c + 1, :]

    low_ids = lax.broadcasted_iota(jnp.int32, (LANES, LANES), 0)

    def vertex_lanes(e, carry):
        for c in range(3):
            lows = ids_ref[c, pl.ds(e, 1), :] & (LANES - 1)
            vert_hot[e, :, c * LANES : (c + 1) * LANES] = (
                (low_ids == lows).astype(F32).astype(BF16)
            )
        return carry

    lax.fori_loop(0, live, vertex_lanes, 0, unroll=2)

    for j in window:
        pos_copies[j].wait_recv()

    sub8 = lax.broadcasted_iota(jnp.int32, (8, LANES), 0)
    shards = 8 // caps
    for q in range(live // 8):
        ids = [ids_ref[c, 8 * q : 8 * q + 8, :] for c in range(3)]
        lows = [x & (LANES - 1) for x in ids]
        highs = [x >> 7 for x in ids]
        sources = []
        for row in range(comps):
            source = None
            for w in range(shards):
                wide = jnp.broadcast_to(pos_all[q * shards + w, row : row + 1, :], (8, LANES))
                source = wide if source is None else jnp.where(sub8 >= w * caps, wide, source)
            sources.append(source)
        for c in range(3):
            masks = [highs[c] == i for i in range(his)]
            for d in range(3):
                picked = jnp.zeros((8, LANES), F32)
                for i in range(his):
                    picked = jnp.where(masks[i], pick_lanes(sources[d * his + i], lows[c]), picked)
                k = c * 3 + d
                table[8 * q : 8 * q + 8, k * LANES : (k + 1) * LANES] = picked

    pick3 = jnp.concatenate([pick, pick, pick], axis=0)
    parts = jnp.concatenate(three_parts(table[...]), axis=0)
    rows_ref[...] = lax.dot_general(pick3, parts, TN, preferred_element_type=F32)

    energy_ref[...] = jnp.zeros((8, LANES), F32)
    loads[10].wait()
    loads[11].wait()

    def shade(g):
        base = pl.multiple_of(g * 8, 8)
        lens = [cam_t[pl.ds(base, 8), i : i + 1] for i in range(12)]
        for half in range(pix // LANES):
            span = slice(half * LANES, (half + 1) * LANES)
            slots = slot_ref[pl.ds(base, 8), span]
            lanes = slots & (BLOCK - 1)
            where_n = slots >> 7
            masks = [where_n == n for n in range(covers)]
            corners = []
            for k in range(9):
                picked = jnp.zeros((8, LANES), F32)
                for n in range(covers):
                    source = rows_ref[
                        pl.ds(pl.multiple_of(n * tiles + base, 8), 8), k * LANES : (k + 1) * LANES
                    ]
                    picked = jnp.where(masks[n], pick_lanes(source, lanes), picked)
                corners.append(picked)
            weights = [bary_ref[c, pl.ds(base, 8), span] for c in range(3)]
            surface = []
            for d in range(3):
                point = weights[0] * corners[d]
                point = point + weights[1] * corners[3 + d]
                surface.append(point + weights[2] * corners[6 + d])
            energy = energy_ref[...]
            grads = []
            for r in range(3):
                linear = lens[3 * r] * surface[0]
                linear = linear + lens[3 * r + 1] * surface[1]
                linear = linear + lens[3 * r + 2] * surface[2]
                shaded = jnp.tanh(linear + lens[9 + r])
                differ = shaded - target_ref[r, pl.ds(base, 8), span]
                square = differ * differ + SMOOTH * SMOOTH
                inverse = lax.rsqrt(square)
                energy = energy + square * inverse
                grads.append(differ * inverse * (1.0 - shaded * shaded))
            energy_ref[...] = energy
            for d in range(3):
                pull = lens[d] * grads[0] + lens[3 + d] * grads[1] + lens[6 + d] * grads[2]
                for c in range(3):
                    value = weights[c] * pull
                    high = value.astype(BF16).astype(F32)
                    corner_grad[c * 3 + d, pl.ds(base, 8), span] = high
                    corner_grad[9 + c * 3 + d, pl.ds(base, 8), span] = value - high

    cover_ids = lax.broadcasted_iota(jnp.int32, (covers, pix), 0)

    def spread_tile(t):
        mine = cover_ids == (slot_ref[pl.ds(t, 1), :] >> 7)
        both = jnp.concatenate(
            [jnp.where(mine, corner_grad[k, pl.ds(t, 1), :], 0.0) for k in range(18)], axis=0
        ).astype(BF16)
        summed = lax.dot_general(both, tile_hot[t], NT, preferred_element_type=F32)
        summed = summed[0 : 9 * covers] + summed[9 * covers :]
        for k in range(9):
            rows_grad[k, pl.ds(t, covers, stride=tiles), :] = summed[k * covers : (k + 1) * covers]

    def spread_group(g):
        for i in range(8):
            spread_tile(g * 8 + i)

    groups = tiles // 8
    shade(0)

    def step(g, carry):
        spread_group(g - 1)
        shade(g)
        return carry

    lax.fori_loop(1, groups, step, 0)
    energy_in[v] = energy_ref[...]
    energy_copies = view_copies(energy_in, energy_send, energy_recv)
    for copy in energy_copies:
        copy.start()
    spread_group(groups - 1)

    pick2 = jnp.concatenate([pick, pick], axis=1)
    for first in range(0, 9, 2):
        ks = range(first, min(first + 2, 9))
        both = jnp.concatenate(
            two_parts(jnp.concatenate([rows_grad[k] for k in ks], axis=1)), axis=0
        )
        summed = jnp.dot(pick2, both, preferred_element_type=F32)
        for i, k in enumerate(ks):
            value = summed[:, i * LANES : (i + 1) * LANES]
            high = value.astype(BF16).astype(F32)
            grad_table[k] = high
            grad_table[9 + k] = value - high

    high_ids = lax.broadcasted_iota(jnp.int32, (his, LANES), 0)

    def shard_grad(j):
        summed = jnp.zeros((2 * comps, LANES), F32)
        for s in range(caps):
            e = j * caps + s
            wide = []
            for c in range(3):
                mine = high_ids == (ids_ref[c, pl.ds(e, 1), :] >> 7)
                wide.append(
                    jnp.concatenate(
                        [
                            jnp.where(mine, grad_table[half + c * 3 + d, pl.ds(e, 1), :], 0.0)
                            for half in (0, 9)
                            for d in range(3)
                        ],
                        axis=0,
                    )
                )
            both = jnp.concatenate(wide, axis=1).astype(BF16)
            summed = summed + lax.dot_general(both, vert_hot[e], NT, preferred_element_type=F32)
        return summed[0:comps] + summed[comps:]

    turns = WIN // nv

    def other_copy(r, m):
        w = at_view(r)
        return pltpu.make_async_remote_copy(
            src_ref=grad_out.at[m * nv + w], dst_ref=view_in.at[v, m],
            send_sem=view_send.at[r, m], recv_sem=view_recv.at[v, m], device_id=(u, w),
            device_id_type=MESH,
        )

    def holder_copy(r, m):
        j = m * nv + v
        step = j - BACK + (j // (WIN - 1)) * (nh // 2 - (WIN - 1 - BACK))
        return pltpu.make_async_remote_copy(
            src_ref=grad_out.at[j], dst_ref=grad_in.at[j], send_sem=grad_send.at[r, m],
            recv_sem=grad_recv.at[j], device_id=(at_vertex(step), at_view(r)),
            device_id_type=MESH,
        )

    for r in range(1, nv):
        grads = [shard_grad(m * nv + at_view(r)) for m in range(turns)]
        for m in range(turns):
            grad_out[m * nv + at_view(r)] = grads[m]
            other_copy(r, m).start()

    grads = [shard_grad(m * nv + v) for m in range(turns)]
    for m in range(turns):
        grad_out[m * nv + v] = grads[m]

    def for_own(m, carry):
        j = m * nv + v
        total = grad_out[j]
        for r in range(1, nv):
            w = at_view(r)
            pltpu.make_async_remote_copy(
                src_ref=view_in.at[w, m], dst_ref=view_in.at[w, m], send_sem=view_recv.at[w, m],
                recv_sem=view_recv.at[w, m], device_id=(u, w), device_id_type=MESH,
            ).wait_recv()
            total = total + view_in[w, m]
        grad_out[j] = total
        for r in range(1, nv):
            holder_copy(r, m).start()

        @pl.when(j != BACK)
        def _():
            holder_copy(0, m).start()

        @pl.when(j == BACK)
        def _():
            grad_in[BACK] = grad_out[BACK]

        return carry

    lax.fori_loop(0, turns, for_own, 0)

    def arrive(j):
        pltpu.make_async_remote_copy(
            src_ref=grad_in.at[j], dst_ref=grad_in.at[j], send_sem=grad_recv.at[j],
            recv_sem=grad_recv.at[j], device_id=(at_vertex(1), v), device_id_type=MESH,
        ).wait_recv()

    @pl.when(v != BACK % nv)
    def _():
        arrive(BACK)

    for j in window:
        arrive(j)
    total = grad_in[0]
    for j in range(1, WIN):
        total = total + grad_in[j]
    for d in range(3):
        for i in range(his):
            vgrad_ref[d : d + 1, i * LANES : (i + 1) * LANES] = total[
                d * his + i : d * his + i + 1, :
            ]

    share = jnp.zeros((2, nk), F32)
    for d in range(3):
        whole = vgrad_ref[d : d + 1, :]
        high = whole.astype(BF16).astype(F32)
        both = jnp.concatenate([high, whole - high], axis=0).astype(BF16)
        share = share + lax.dot_general(both, basis_v[d], NT, preferred_element_type=F32)
    share = share[0:1] + share[1:2]
    wide = min(nk, LANES)
    rows = nk // wide
    coeff_in[u] = jnp.zeros((8, LANES), F32)
    for i in range(rows):
        coeff_in[u, i : i + 1, 0:wide] = share[:, i * wide : (i + 1) * wide]
    wait_views(energy_in, energy_recv)
    energy = energy_in[0]
    for other in range(1, nv):
        energy = energy + energy_in[other]
    coeff_in[u, rows : rows + 1, :] = jnp.sum(energy, axis=0, keepdims=True)
    coeff_copies = []
    for r in sorted(range(1, nh), key=lambda r: abs(r - nh // 2)):
        coeff_copies.append(
            pltpu.make_async_remote_copy(
                src_ref=coeff_in.at[u], dst_ref=coeff_in.at[u], send_sem=coeff_send.at[r],
                recv_sem=coeff_recv.at[u], device_id=(at_vertex(r), v), device_id_type=MESH,
            )
        )
        coeff_copies[-1].start()

    for copies in (tri_copies, pos_copies):
        for j in window:
            copies[j].wait_send()
    for copy in part_copies + energy_copies:
        copy.wait_send()

    def sent(m, carry):
        for r in range(1, nv):
            other_copy(r, m).wait_send()
            holder_copy(r, m).wait_send()

        @pl.when(m * nv + v != BACK)
        def _():
            holder_copy(0, m).wait_send()

        return carry

    lax.fori_loop(0, turns, sent, 0)
    for r in range(1, nh):
        other = at_vertex(r)
        pltpu.make_async_remote_copy(
            src_ref=coeff_in.at[other], dst_ref=coeff_in.at[other], send_sem=coeff_recv.at[other],
            recv_sem=coeff_recv.at[other], device_id=(other, v), device_id_type=MESH,
        ).wait_recv()
    total = coeff_in[0]
    for other in range(1, nh):
        total = total + coeff_in[other]
    sums_ref[...] = total
    for copy in coeff_copies:
        copy.wait_send()


def finish(pixel_total, gathered_ref, sums_ref, loss_ref, vgrad_ref, coeff_ref):
    nk = coeff_ref.shape[1]
    wide = min(nk, LANES)
    rows = nk // wide
    vgrad_ref[...] = gathered_ref[...]
    for i in range(rows):
        coeff_ref[:, i * wide : (i + 1) * wide] = sums_ref[i : i + 1, 0:wide]
    energy = jnp.sum(sums_ref[rows : rows + 1, :], axis=1, keepdims=True)
    loss_ref[...] = energy / pixel_total


def per_device(
    nh, nv, coeffs, shape_basis, rest_pose, triangles, fetch_list, tile_cover, pix_slot,
    barycentric, camera, target,
):
    nk, _, verts = shape_basis.shape
    tiles, pix = pix_slot.shape
    covers = tile_cover.shape[1]
    caps = fetch_list.shape[2]
    live = WIN * caps
    comps = 3 * verts // LANES
    vmem = pl.BlockSpec(memory_space=pltpu.VMEM)
    hbm = pl.BlockSpec(memory_space=pl.ANY)
    dma = pltpu.SemaphoreType.DMA
    gathered, sums = pl.pallas_call(
        functools.partial(kernel, nh, nv),
        out_shape=(
            jax.ShapeDtypeStruct((3, verts), F32),
            jax.ShapeDtypeStruct((8, LANES), F32),
        ),
        in_specs=[hbm] * 10,
        out_specs=(vmem, vmem),
        scratch_shapes=[
            pltpu.VMEM((nk,), BF16),
            pltpu.VMEM((3, nk, verts), BF16),
            pltpu.VMEM((3, verts), F32),
            pltpu.SMEM((caps, nh), jnp.int32),
            pltpu.VMEM((covers, tiles), jnp.int32),
            pltpu.VMEM((tiles, pix), jnp.int32),
            pltpu.VMEM((3, tiles, pix), F32),
            pltpu.VMEM((12, tiles), F32),
            pltpu.VMEM((3, tiles, pix), F32),
            pltpu.VMEM((tiles, BLOCK, pix), BF16),
            pltpu.VMEM((live, LANES, 3 * LANES), BF16),
            pltpu.VMEM((nv, comps, LANES), F32),
            pltpu.VMEM((comps, LANES), F32),
            pltpu.VMEM((WIN, comps, LANES), F32),
            pltpu.VMEM((WIN,) + triangles.shape, jnp.int32),
            pltpu.VMEM((3, live, LANES), jnp.int32),
            pltpu.VMEM((live, 9 * LANES), F32),
            pltpu.VMEM((1, covers * tiles), jnp.int32),
            pltpu.VMEM((covers * tiles, 9 * LANES), F32),
            pltpu.VMEM((tiles, 12), F32),
            pltpu.VMEM((18, tiles, pix), F32),
            pltpu.VMEM((9, covers * tiles, LANES), F32),
            pltpu.VMEM((8, LANES), F32),
            pltpu.VMEM((18, live, LANES), F32),
            pltpu.VMEM((WIN, comps, LANES), F32),
            pltpu.VMEM((WIN, comps, LANES), F32),
            pltpu.VMEM((nv, WIN // nv, comps, LANES), F32),
            pltpu.VMEM((nv, 8, LANES), F32),
            pltpu.VMEM((nh, 8, LANES), F32),
            dma((12,)),
            dma((WIN,)), dma((WIN,)),
            dma((nv,)), dma((nv,)),
            dma((WIN,)), dma((WIN,)),
            dma((nv, WIN // nv)), dma((WIN,)),
            dma((nv, WIN // nv)), dma((nv, WIN // nv)),
            dma((nv,)), dma((nv,)),
            dma((nh,)), dma((nh,)),
        ],
        compiler_params=pltpu.CompilerParams(
            collective_id=0, has_side_effects=True, vmem_limit_bytes=62 * 1024 * 1024
        ),
    )(
        coeffs,
        jnp.transpose(shape_basis, (1, 0, 2)),
        rest_pose,
        triangles,
        jnp.transpose(fetch_list[0], (1, 0)),
        jnp.transpose(tile_cover, (1, 0)),
        pix_slot,
        jnp.transpose(barycentric, (1, 0, 2)),
        jnp.transpose(camera, (1, 0)),
        jnp.transpose(target, (1, 0, 2)),
    )
    loss, vertex_grad, coeff_grad = pl.pallas_call(
        functools.partial(finish, float(tiles * pix * nh * nv)),
        out_shape=(
            jax.ShapeDtypeStruct((1, 1), F32),
            jax.ShapeDtypeStruct((3, verts), F32),
            jax.ShapeDtypeStruct((1, nk), F32),
        ),
        in_specs=[vmem, vmem],
        out_specs=(vmem, vmem, vmem),
        compiler_params=pltpu.CompilerParams(vmem_limit_bytes=62 * 1024 * 1024),
    )(gathered, sums)
    return loss.reshape(()), vertex_grad, coeff_grad.reshape(nk)


def solution(mesh):
    placed = (
        P("view"),
        P("view", None, "vertex"),
        P(None, "vertex"),
        P(None, "vertex"),
        P(("vertex", "view"), None, None),
        P(("vertex", "view"), None),
        P(("vertex", "view"), None),
        P(("vertex", "view"), None, None),
        P(("vertex", "view"), None),
        P(("vertex", "view"), None, None),
    )
    return jax.shard_map(
        functools.partial(per_device, mesh.shape["vertex"], mesh.shape["view"]),
        mesh=mesh,
        in_specs=placed,
        out_specs=(P(), P(None, "vertex"), P("view")),
        check_vma=False,
    )
```

```python
import functools

import jax
import jax.numpy as jnp
from jax import lax
from jax.experimental import pallas as pl
from jax.experimental.pallas import tpu as pltpu
from jax.sharding import PartitionSpec as P

MESH = pl.DeviceIdType.MESH
BLOCK = 128
LANES = 128
WIN = 8
BACK = 3
SMOOTH = 0.1
F32 = jnp.float32
BF16 = jnp.bfloat16
NT = (((1,), (1,)), ((), ()))
TN = (((0,), (0,)), ((), ()))


def reach(j, holders):
    return holders // 2 if j == WIN - 1 else j - BACK


def pick_lanes(table, lanes):
    return jnp.take_along_axis(table, lanes, axis=1, mode="promise_in_bounds")


def two_parts(values):
    high = values.astype(BF16)
    low = (values - high.astype(F32)).astype(BF16)
    return high, low


def three_parts(values):
    high = values.astype(BF16)
    rest = values - high.astype(F32)
    middle = rest.astype(BF16)
    low = (rest - middle.astype(F32)).astype(BF16)
    return high, middle, low


def kernel(
    nh, nv,
    coeffs_in, basis_in, rest_in, tri_ref, fetch_in, cover_in, slot_in, bary_in, cam_in, target_in,
    vgrad_ref, sums_ref,
    coeffs_ref, basis_v, rest_ref, fetch_ref, cover_ref, slot_ref, bary_ref, cam_ref, target_ref,
    tile_hot, vert_hot, part, rest_rows, pos_all, tri_all, ids_ref, table, cover_row, rows_ref, cam_t,
    corner_grad, rows_grad, energy_ref, grad_table, grad_out, grad_in, view_in, energy_in,
    coeff_in,
    load_sem, tri_send, tri_recv, share_send, share_recv, part_send, part_recv, pos_send, pos_recv, grad_send, grad_recv,
    view_send, view_recv, energy_send, energy_recv, coeff_send, coeff_recv,
):
    u = lax.axis_index("vertex")
    v = lax.axis_index("view")
    nk = basis_v.shape[1]
    his = rest_ref.shape[1] // LANES
    comps = 3 * his
    tiles = slot_ref.shape[0]
    pix = slot_ref.shape[1]
    covers = cover_ref.shape[0]
    caps = fetch_ref.shape[0]
    cap_bits = caps.bit_length() - 1
    live = WIN * caps
    window = [j for j in range(WIN) if j != BACK]

    def at_vertex(step):
        return lax.rem(u + step + nh, nh)

    def at_view(step):
        return lax.rem(v + step, nv)

    width = tri_ref.shape[1] // nv

    def share_of(view):
        return pl.ds(pl.multiple_of(view * width, width), width)

    mine = share_of(v)
    pairs = [
        (coeffs_in, coeffs_ref), (basis_in.at[0], basis_v.at[0]), (basis_in.at[1], basis_v.at[1]),
        (basis_in.at[2], basis_v.at[2]), (rest_in, rest_ref), (cover_in, cover_ref),
        (cam_in, cam_ref), (slot_in, slot_ref), (fetch_in, fetch_ref),
        (tri_ref.at[:, mine], tri_all.at[BACK, :, mine]),
        (bary_in, bary_ref), (target_in, target_ref),
    ]
    loads = [
        pltpu.make_async_copy(src, dst, load_sem.at[i]) for i, (src, dst) in enumerate(pairs)
    ]
    barrier = pltpu.get_barrier_semaphore()
    for r in range(1, nv):
        pl.semaphore_signal(barrier, inc=1, device_id=(u, at_view(r)), device_id_type=MESH)
    for r in sorted(range(1, nh), key=lambda r: abs(r - nh // 2)):
        pl.semaphore_signal(barrier, inc=1, device_id=(at_vertex(r), v), device_id_type=MESH)
    for load in loads:
        load.start()

    loads[0].wait()
    for d in range(3):
        loads[1 + d].wait()
        share = jnp.dot(coeffs_ref[...].reshape(1, nk), basis_v[d], preferred_element_type=F32)
        for i in range(his):
            part[v, pl.ds(d * his + i, 1), :] = share[:, i * LANES : (i + 1) * LANES]

    pl.semaphore_wait(barrier, nh + nv - 2)

    def view_copies(buffer, send, recv):
        out = []
        for r in range(1, nv):
            out.append(
                pltpu.make_async_remote_copy(
                    src_ref=buffer.at[v], dst_ref=buffer.at[v], send_sem=send.at[r],
                    recv_sem=recv.at[v], device_id=(u, at_view(r)), device_id_type=MESH,
                )
            )
        return out

    def wait_views(buffer, recv):
        for r in range(1, nv):
            other = at_view(r)
            pltpu.make_async_remote_copy(
                src_ref=buffer.at[other], dst_ref=buffer.at[other], send_sem=recv.at[other],
                recv_sem=recv.at[other], device_id=(u, other), device_id_type=MESH,
            ).wait_recv()

    part_copies = view_copies(part, part_send, part_recv)
    for copy in part_copies:
        copy.start()
    tri_copies = {}
    for j in window:
        tri_copies[j] = pltpu.make_async_remote_copy(
            src_ref=tri_ref.at[:, mine], dst_ref=tri_all.at[j, :, mine], send_sem=tri_send.at[j],
            recv_sem=tri_recv.at[j], device_id=(at_vertex(-reach(j, nh)), v), device_id_type=MESH,
        )
        tri_copies[j].start()

    for load in loads[4:8]:
        load.wait()
    for d in range(3):
        for i in range(his):
            rest_rows[d * his + i : d * his + i + 1, :] = rest_ref[
                d : d + 1, i * LANES : (i + 1) * LANES
            ]
    entry = cover_ref[...]
    holder = entry >> cap_bits
    away = holder - u
    away = jnp.where(away < 0, away + nh, away)
    near = jnp.where(away <= BACK, away + BACK, away + BACK - nh)
    compact = jnp.where(away == nh // 2, WIN - 1, near) * caps + (entry & (caps - 1))
    for n in range(covers):
        cover_row[0:1, n * tiles : (n + 1) * tiles] = compact[n : n + 1, :]
    entry_ids = lax.broadcasted_iota(jnp.int32, (live, covers * tiles), 0)
    pick = (entry_ids == cover_row[...]).astype(F32).astype(BF16)
    cam_t[...] = jnp.transpose(cam_ref[...])

    lane_ids = lax.broadcasted_iota(jnp.int32, (BLOCK, pix), 0)

    def tile_lanes(t, carry):
        lanes = slot_ref[pl.ds(t, 1), :] & (BLOCK - 1)
        tile_hot[t] = (lane_ids == lanes).astype(F32).astype(BF16)
        return carry

    wait_views(part, part_recv)
    total = part[0]
    for other in range(1, nv):
        total = total + part[other]
    pos_all[BACK] = rest_rows[...] + total
    pos_copies = {}
    for j in window:
        pos_copies[j] = pltpu.make_async_remote_copy(
            src_ref=pos_all.at[BACK], dst_ref=pos_all.at[j], send_sem=pos_send.at[j],
            recv_sem=pos_recv.at[j], device_id=(at_vertex(-reach(j, nh)), v), device_id_type=MESH,
        )
        pos_copies[j].start()

    share_copies = []
    loads[8].wait()
    loads[9].wait()
    for j in window:
        tri_copies[j].wait_recv()
    for r in range(1, nv):
        share_copies.append(
            pltpu.make_async_remote_copy(
                src_ref=tri_all.at[:, :, mine], dst_ref=tri_all.at[:, :, mine],
                send_sem=share_send.at[r], recv_sem=share_recv.at[v], device_id=(u, at_view(r)),
                device_id_type=MESH,
            )
        )
        share_copies[-1].start()
    lax.fori_loop(0, tiles, tile_lanes, 0, unroll=4)
    for r in range(1, nv):
        other = at_view(r)
        theirs = tri_all.at[:, :, share_of(other)]
        pltpu.make_async_remote_copy(
            src_ref=theirs, dst_ref=theirs, send_sem=share_recv.at[other],
            recv_sem=share_recv.at[other], device_id=(u, other), device_id_type=MESH,
        ).wait_recv()
    blocks = tri_ref.shape[1] // BLOCK
    for j in range(WIN):
        wanted = [
            jnp.full((3, BLOCK), fetch_ref[s, at_vertex(reach(j, nh))], jnp.int32)
            for s in range(caps)
        ]
        found = [jnp.zeros((3, BLOCK), jnp.int32)] * caps
        for b in range(blocks):
            corners = tri_all[j, :, b * BLOCK : (b + 1) * BLOCK]
            for s in range(caps):
                found[s] = jnp.where(wanted[s] == b, corners, found[s])
        for s in range(caps):
            for c in range(3):
                ids_ref[c, j * caps + s : j * caps + s + 1, :] = found[s][c : c + 1, :]

    low_ids = lax.broadcasted_iota(jnp.int32, (LANES, LANES), 0)

    def vertex_lanes(e, carry):
        for c in range(3):
            lows = ids_ref[c, pl.ds(e, 1), :] & (LANES - 1)
            vert_hot[e, :, c * LANES : (c + 1) * LANES] = (
                (low_ids == lows).astype(F32).astype(BF16)
            )
        return carry

    lax.fori_loop(0, live, vertex_lanes, 0, unroll=2)

    for j in window:
        pos_copies[j].wait_recv()

    sub8 = lax.broadcasted_iota(jnp.int32, (8, LANES), 0)
    shards = 8 // caps
    for q in range(live // 8):
        ids = [ids_ref[c, 8 * q : 8 * q + 8, :] for c in range(3)]
        lows = [x & (LANES - 1) for x in ids]
        highs = [x >> 7 for x in ids]
        sources = []
        for row in range(comps):
            source = None
            for w in range(shards):
                wide = jnp.broadcast_to(pos_all[q * shards + w, row : row + 1, :], (8, LANES))
                source = wide if source is None else jnp.where(sub8 >= w * caps, wide, source)
            sources.append(source)
        for c in range(3):
            masks = [highs[c] == i for i in range(his)]
            for d in range(3):
                picked = jnp.zeros((8, LANES), F32)
                for i in range(his):
                    picked = jnp.where(masks[i], pick_lanes(sources[d * his + i], lows[c]), picked)
                k = c * 3 + d
                table[8 * q : 8 * q + 8, k * LANES : (k + 1) * LANES] = picked

    pick3 = jnp.concatenate([pick, pick, pick], axis=0)
    parts = jnp.concatenate(three_parts(table[...]), axis=0)
    rows_ref[...] = lax.dot_general(pick3, parts, TN, preferred_element_type=F32)

    energy_ref[...] = jnp.zeros((8, LANES), F32)
    loads[10].wait()
    loads[11].wait()

    def shade(g):
        base = pl.multiple_of(g * 8, 8)
        lens = [cam_t[pl.ds(base, 8), i : i + 1] for i in range(12)]
        for half in range(pix // LANES):
            span = slice(half * LANES, (half + 1) * LANES)
            slots = slot_ref[pl.ds(base, 8), span]
            lanes = slots & (BLOCK - 1)
            where_n = slots >> 7
            masks = [where_n == n for n in range(covers)]
            corners = []
            for k in range(9):
                picked = jnp.zeros((8, LANES), F32)
                for n in range(covers):
                    source = rows_ref[
                        pl.ds(pl.multiple_of(n * tiles + base, 8), 8), k * LANES : (k + 1) * LANES
                    ]
                    picked = jnp.where(masks[n], pick_lanes(source, lanes), picked)
                corners.append(picked)
            weights = [bary_ref[c, pl.ds(base, 8), span] for c in range(3)]
            surface = []
            for d in range(3):
                point = weights[0] * corners[d]
                point = point + weights[1] * corners[3 + d]
                surface.append(point + weights[2] * corners[6 + d])
            energy = energy_ref[...]
            grads = []
            for r in range(3):
                linear = lens[3 * r] * surface[0]
                linear = linear + lens[3 * r + 1] * surface[1]
                linear = linear + lens[3 * r + 2] * surface[2]
                shaded = jnp.tanh(linear + lens[9 + r])
                differ = shaded - target_ref[r, pl.ds(base, 8), span]
                square = differ * differ + SMOOTH * SMOOTH
                inverse = lax.rsqrt(square)
                energy = energy + square * inverse
                grads.append(differ * inverse * (1.0 - shaded * shaded))
            energy_ref[...] = energy
            for d in range(3):
                pull = lens[d] * grads[0] + lens[3 + d] * grads[1] + lens[6 + d] * grads[2]
                for c in range(3):
                    value = weights[c] * pull
                    high = value.astype(BF16).astype(F32)
                    corner_grad[c * 3 + d, pl.ds(base, 8), span] = high
                    corner_grad[9 + c * 3 + d, pl.ds(base, 8), span] = value - high

    cover_ids = lax.broadcasted_iota(jnp.int32, (covers, pix), 0)

    def spread_tile(t):
        mine = cover_ids == (slot_ref[pl.ds(t, 1), :] >> 7)
        both = jnp.concatenate(
            [jnp.where(mine, corner_grad[k, pl.ds(t, 1), :], 0.0) for k in range(18)], axis=0
        ).astype(BF16)
        summed = lax.dot_general(both, tile_hot[t], NT, preferred_element_type=F32)
        summed = summed[0 : 9 * covers] + summed[9 * covers :]
        for k in range(9):
            rows_grad[k, pl.ds(t, covers, stride=tiles), :] = summed[k * covers : (k + 1) * covers]

    def spread_group(g):
        for i in range(8):
            spread_tile(g * 8 + i)

    groups = tiles // 8
    shade(0)

    def step(g, carry):
        spread_group(g - 1)
        shade(g)
        return carry

    lax.fori_loop(1, groups, step, 0)
    energy_in[v] = energy_ref[...]
    energy_copies = view_copies(energy_in, energy_send, energy_recv)
    for copy in energy_copies:
        copy.start()
    spread_group(groups - 1)

    pick2 = jnp.concatenate([pick, pick], axis=1)
    for first in range(0, 9, 2):
        ks = range(first, min(first + 2, 9))
        both = jnp.concatenate(
            two_parts(jnp.concatenate([rows_grad[k] for k in ks], axis=1)), axis=0
        )
        summed = jnp.dot(pick2, both, preferred_element_type=F32)
        for i, k in enumerate(ks):
            value = summed[:, i * LANES : (i + 1) * LANES]
            high = value.astype(BF16).astype(F32)
            grad_table[k] = high
            grad_table[9 + k] = value - high

    high_ids = lax.broadcasted_iota(jnp.int32, (his, LANES), 0)

    def shard_grad(j):
        summed = jnp.zeros((2 * comps, LANES), F32)
        for s in range(caps):
            e = j * caps + s
            wide = []
            for c in range(3):
                mine = high_ids == (ids_ref[c, pl.ds(e, 1), :] >> 7)
                wide.append(
                    jnp.concatenate(
                        [
                            jnp.where(mine, grad_table[half + c * 3 + d, pl.ds(e, 1), :], 0.0)
                            for half in (0, 9)
                            for d in range(3)
                        ],
                        axis=0,
                    )
                )
            both = jnp.concatenate(wide, axis=1).astype(BF16)
            summed = summed + lax.dot_general(both, vert_hot[e], NT, preferred_element_type=F32)
        return summed[0:comps] + summed[comps:]

    turns = WIN // nv

    def other_copy(r, m):
        w = at_view(r)
        return pltpu.make_async_remote_copy(
            src_ref=grad_out.at[m * nv + w], dst_ref=view_in.at[v, m],
            send_sem=view_send.at[r, m], recv_sem=view_recv.at[v, m], device_id=(u, w),
            device_id_type=MESH,
        )

    def holder_copy(r, m):
        j = m * nv + v
        step = j - BACK + (j // (WIN - 1)) * (nh // 2 - (WIN - 1 - BACK))
        return pltpu.make_async_remote_copy(
            src_ref=grad_out.at[j], dst_ref=grad_in.at[j], send_sem=grad_send.at[r, m],
            recv_sem=grad_recv.at[j], device_id=(at_vertex(step), at_view(r)),
            device_id_type=MESH,
        )

    for r in range(1, nv):
        grads = [shard_grad(m * nv + at_view(r)) for m in range(turns)]
        for m in range(turns):
            grad_out[m * nv + at_view(r)] = grads[m]
            other_copy(r, m).start()

    grads = [shard_grad(m * nv + v) for m in range(turns)]
    for m in range(turns):
        grad_out[m * nv + v] = grads[m]

    def for_own(m, carry):
        j = m * nv + v
        total = grad_out[j]
        for r in range(1, nv):
            w = at_view(r)
            pltpu.make_async_remote_copy(
                src_ref=view_in.at[w, m], dst_ref=view_in.at[w, m], send_sem=view_recv.at[w, m],
                recv_sem=view_recv.at[w, m], device_id=(u, w), device_id_type=MESH,
            ).wait_recv()
            total = total + view_in[w, m]
        grad_out[j] = total
        for r in range(1, nv):
            holder_copy(r, m).start()

        @pl.when(j != BACK)
        def _():
            holder_copy(0, m).start()

        @pl.when(j == BACK)
        def _():
            grad_in[BACK] = grad_out[BACK]

        return carry

    lax.fori_loop(0, turns, for_own, 0)

    def arrive(j):
        pltpu.make_async_remote_copy(
            src_ref=grad_in.at[j], dst_ref=grad_in.at[j], send_sem=grad_recv.at[j],
            recv_sem=grad_recv.at[j], device_id=(at_vertex(1), v), device_id_type=MESH,
        ).wait_recv()

    @pl.when(v != BACK % nv)
    def _():
        arrive(BACK)

    for j in window:
        arrive(j)
    total = grad_in[0]
    for j in range(1, WIN):
        total = total + grad_in[j]
    for d in range(3):
        for i in range(his):
            vgrad_ref[d : d + 1, i * LANES : (i + 1) * LANES] = total[
                d * his + i : d * his + i + 1, :
            ]

    share = jnp.zeros((2, nk), F32)
    for d in range(3):
        whole = vgrad_ref[d : d + 1, :]
        high = whole.astype(BF16).astype(F32)
        both = jnp.concatenate([high, whole - high], axis=0).astype(BF16)
        share = share + lax.dot_general(both, basis_v[d], NT, preferred_element_type=F32)
    share = share[0:1] + share[1:2]
    wide = min(nk, LANES)
    rows = nk // wide
    coeff_in[u] = jnp.zeros((8, LANES), F32)
    for i in range(rows):
        coeff_in[u, i : i + 1, 0:wide] = share[:, i * wide : (i + 1) * wide]
    wait_views(energy_in, energy_recv)
    energy = energy_in[0]
    for other in range(1, nv):
        energy = energy + energy_in[other]
    coeff_in[u, rows : rows + 1, :] = jnp.sum(energy, axis=0, keepdims=True)
    coeff_copies = []
    for r in sorted(range(1, nh), key=lambda r: abs(r - nh // 2)):
        coeff_copies.append(
            pltpu.make_async_remote_copy(
                src_ref=coeff_in.at[u], dst_ref=coeff_in.at[u], send_sem=coeff_send.at[r],
                recv_sem=coeff_recv.at[u], device_id=(at_vertex(r), v), device_id_type=MESH,
            )
        )
        coeff_copies[-1].start()

    for copies in (tri_copies, pos_copies):
        for j in window:
            copies[j].wait_send()
    for copy in part_copies + share_copies + energy_copies:
        copy.wait_send()

    def sent(m, carry):
        for r in range(1, nv):
            other_copy(r, m).wait_send()
            holder_copy(r, m).wait_send()

        @pl.when(m * nv + v != BACK)
        def _():
            holder_copy(0, m).wait_send()

        return carry

    lax.fori_loop(0, turns, sent, 0)
    for r in range(1, nh):
        other = at_vertex(r)
        pltpu.make_async_remote_copy(
            src_ref=coeff_in.at[other], dst_ref=coeff_in.at[other], send_sem=coeff_recv.at[other],
            recv_sem=coeff_recv.at[other], device_id=(other, v), device_id_type=MESH,
        ).wait_recv()
    total = coeff_in[0]
    for other in range(1, nh):
        total = total + coeff_in[other]
    sums_ref[...] = total
    for copy in coeff_copies:
        copy.wait_send()


def finish(pixel_total, gathered_ref, sums_ref, loss_ref, vgrad_ref, coeff_ref):
    nk = coeff_ref.shape[1]
    wide = min(nk, LANES)
    rows = nk // wide
    vgrad_ref[...] = gathered_ref[...]
    for i in range(rows):
        coeff_ref[:, i * wide : (i + 1) * wide] = sums_ref[i : i + 1, 0:wide]
    energy = jnp.sum(sums_ref[rows : rows + 1, :], axis=1, keepdims=True)
    loss_ref[...] = energy / pixel_total


def per_device(
    nh, nv, coeffs, shape_basis, rest_pose, triangles, fetch_list, tile_cover, pix_slot,
    barycentric, camera, target,
):
    nk, _, verts = shape_basis.shape
    tiles, pix = pix_slot.shape
    covers = tile_cover.shape[1]
    caps = fetch_list.shape[2]
    live = WIN * caps
    comps = 3 * verts // LANES
    vmem = pl.BlockSpec(memory_space=pltpu.VMEM)
    hbm = pl.BlockSpec(memory_space=pl.ANY)
    dma = pltpu.SemaphoreType.DMA
    gathered, sums = pl.pallas_call(
        functools.partial(kernel, nh, nv),
        out_shape=(
            jax.ShapeDtypeStruct((3, verts), F32),
            jax.ShapeDtypeStruct((8, LANES), F32),
        ),
        in_specs=[hbm] * 10,
        out_specs=(vmem, vmem),
        scratch_shapes=[
            pltpu.VMEM((nk,), BF16),
            pltpu.VMEM((3, nk, verts), BF16),
            pltpu.VMEM((3, verts), F32),
            pltpu.SMEM((caps, nh), jnp.int32),
            pltpu.VMEM((covers, tiles), jnp.int32),
            pltpu.VMEM((tiles, pix), jnp.int32),
            pltpu.VMEM((3, tiles, pix), F32),
            pltpu.VMEM((12, tiles), F32),
            pltpu.VMEM((3, tiles, pix), F32),
            pltpu.VMEM((tiles, BLOCK, pix), BF16),
            pltpu.VMEM((live, LANES, 3 * LANES), BF16),
            pltpu.VMEM((nv, comps, LANES), F32),
            pltpu.VMEM((comps, LANES), F32),
            pltpu.VMEM((WIN, comps, LANES), F32),
            pltpu.VMEM((WIN,) + triangles.shape, jnp.int32),
            pltpu.VMEM((3, live, LANES), jnp.int32),
            pltpu.VMEM((live, 9 * LANES), F32),
            pltpu.VMEM((1, covers * tiles), jnp.int32),
            pltpu.VMEM((covers * tiles, 9 * LANES), F32),
            pltpu.VMEM((tiles, 12), F32),
            pltpu.VMEM((18, tiles, pix), F32),
            pltpu.VMEM((9, covers * tiles, LANES), F32),
            pltpu.VMEM((8, LANES), F32),
            pltpu.VMEM((18, live, LANES), F32),
            pltpu.VMEM((WIN, comps, LANES), F32),
            pltpu.VMEM((WIN, comps, LANES), F32),
            pltpu.VMEM((nv, WIN // nv, comps, LANES), F32),
            pltpu.VMEM((nv, 8, LANES), F32),
            pltpu.VMEM((nh, 8, LANES), F32),
            dma((12,)),
            dma((WIN,)), dma((WIN,)),
            dma((nv,)), dma((nv,)),
            dma((nv,)), dma((nv,)),
            dma((WIN,)), dma((WIN,)),
            dma((nv, WIN // nv)), dma((WIN,)),
            dma((nv, WIN // nv)), dma((nv, WIN // nv)),
            dma((nv,)), dma((nv,)),
            dma((nh,)), dma((nh,)),
        ],
        compiler_params=pltpu.CompilerParams(
            collective_id=0, has_side_effects=True, vmem_limit_bytes=62 * 1024 * 1024
        ),
    )(
        coeffs,
        jnp.transpose(shape_basis, (1, 0, 2)),
        rest_pose,
        triangles,
        jnp.transpose(fetch_list[0], (1, 0)),
        jnp.transpose(tile_cover, (1, 0)),
        pix_slot,
        jnp.transpose(barycentric, (1, 0, 2)),
        jnp.transpose(camera, (1, 0)),
        jnp.transpose(target, (1, 0, 2)),
    )
    loss, vertex_grad, coeff_grad = pl.pallas_call(
        functools.partial(finish, float(tiles * pix * nh * nv)),
        out_shape=(
            jax.ShapeDtypeStruct((1, 1), F32),
            jax.ShapeDtypeStruct((3, verts), F32),
            jax.ShapeDtypeStruct((1, nk), F32),
        ),
        in_specs=[vmem, vmem],
        out_specs=(vmem, vmem, vmem),
        compiler_params=pltpu.CompilerParams(vmem_limit_bytes=62 * 1024 * 1024),
    )(gathered, sums)
    return loss.reshape(()), vertex_grad, coeff_grad.reshape(nk)


def solution(mesh):
    placed = (
        P("view"),
        P("view", None, "vertex"),
        P(None, "vertex"),
        P(None, "vertex"),
        P(("vertex", "view"), None, None),
        P(("vertex", "view"), None),
        P(("vertex", "view"), None),
        P(("vertex", "view"), None, None),
        P(("vertex", "view"), None),
        P(("vertex", "view"), None, None),
    )
    return jax.shard_map(
        functools.partial(per_device, mesh.shape["vertex"], mesh.shape["view"]),
        mesh=mesh,
        in_specs=placed,
        out_specs=(P(), P(None, "vertex"), P("view")),
        check_vma=False,
    )
```
